32 devices in a mesh: grp: 2 (over x), tile: 16 (over z, y, core).
Axes of the slice: x: 2, y: 2, z: 4, core: 2. Of those that a mesh axis runs over, the one named last changes fastest.
Arguments:
- x_tiles: bfloat16 [32, 16, 16, 256], P(('grp', 'tile')), parts along dimension 0, may hold values from -6 to 6
- h_tiles: bfloat16 [32, 16, 16, 256], P(('grp', 'tile')), parts along dimension 0, may hold values from -6 to 6
- grad_out: bfloat16 [32, 16, 16, 256], P(('grp', 'tile')), parts along dimension 0, may hold values from -6 to 6
- w_gate: bfloat16 [4608, 512], replicated, may hold values from -0.09375 to 0.09375
- b_gate: float32 [512], replicated, may hold values from -3 to 3
- w_cand: bfloat16 [4608, 256], replicated, may hold values from -0.09375 to 0.09375
- b_cand: float32 [256], replicated, may hold values from -3 to 3
- partner_edge: int32 [16, 4], replicated, may hold values from 0 to 63, as said below
- edge_flip: int32 [16, 4], replicated, may hold values from 0 to 1, as said below
- tile_slot: int32 [16], replicated, may hold values from 0 to 15, as said below
Outputs:
- grad_x: bfloat16 [32, 16, 16, 256], P(('grp', 'tile')), parts along dimension 0
- grad_h: bfloat16 [32, 16, 16, 256], P(('grp', 'tile')), parts along dimension 0
- grad_w_gate: float32 [9216, 512], P(('grp', 'tile')), parts along dimension 0
- grad_w_cand: float32 [9216, 256], P(('grp', 'tile')), parts along dimension 0
The draws below stay inside these ranges and needn't reach their ends.
There are 2 independent parts, one for each index of `grp`. The reference program is written for one: setup_inputs(seed, part) draws one part's arguments, and reference() takes and returns one part's arrays. A program takes and returns all parts, laid end to end along the dimension named above; an argument that names none is the same for every part. Nothing has to cross between parts.
Inputs may be any that keep to these rules, and one draw needn't show every extreme that they name: `partner_edge`: the matching is an involution over all 64 tile edges and never joins a tile to itself; of each tile's four edges, two meet edges of the tile in the next slot and two meet edges of the tile in the previous slot, slots counted cyclically. `edge_flip`: equal at both edges of a matched pair. `tile_slot`: A permutation of the slots.
All inputs are finite; a program needn't handle non-finite values.
Results may differ from the reference program's by a relative error of at most 0.0051.
Values may be sent and summed in bfloat16 or wider, within the bound.
No kernel may reach another device: no remote copies, remote signals or barrier semaphores. Data moves between devices by JAX's collectives and lax.ppermute only.
A program may use at most 128 MiB of HBM per device.

```python
import jax
import jax.numpy as jnp

C = 256
S = 16
TILES = 16


def matching(base_key):
    tile_count = TILES
    key_order, key_flip, key_slot = jax.random.split(jax.random.fold_in(base_key, 7), 3)
    orders = jax.vmap(lambda sub_key: jax.random.permutation(sub_key, 4))(jax.random.split(key_order, tile_count)).astype(jnp.int32)
    slot_ids = jnp.arange(tile_count, dtype=jnp.int32)
    next_slot = (slot_ids + 1) % tile_count
    right_ends = (slot_ids[:, None] * 4 + orders[:, :2]).reshape(-1)
    left_ends = (next_slot[:, None] * 4 + orders[next_slot][:, 2:]).reshape(-1)
    partner_of = jnp.zeros((4 * tile_count,), jnp.int32).at[right_ends].set(left_ends).at[left_ends].set(right_ends)
    flip_draw = jax.random.randint(key_flip, (2 * tile_count,), 0, 2, dtype=jnp.int32)
    flip_table = jnp.zeros((4 * tile_count,), jnp.int32).at[right_ends].set(flip_draw).at[left_ends].set(flip_draw)
    tile_slot = jax.random.permutation(key_slot, tile_count).astype(jnp.int32)
    holder = jnp.zeros((tile_count,), jnp.int32).at[tile_slot].set(slot_ids)
    edge_ids = tile_slot[:, None] * 4 + jnp.arange(4, dtype=jnp.int32)[None, :]
    partners = partner_of[edge_ids]
    partner_tile = holder[partners // 4] * 4 + partners % 4
    return (partner_tile.astype(jnp.int32), flip_table[edge_ids], tile_slot)


def draw_partner_edge(key, part):
    return matching(key)[0]


def draw_edge_flip(key, part):
    return matching(key)[1]


def draw_tile_slot(key, part):
    return matching(key)[2]


def steps_of(own_key, extent, cuts, least, top_value):
    def one(axis_at, blocks):
        draws = jax.random.uniform(jax.random.fold_in(jax.random.fold_in(own_key, 6), axis_at), (blocks,), jnp.float32, least / len(cuts), top_value / len(cuts))
        return jnp.repeat(jnp.exp(draws), extent[axis_at] // blocks).reshape((-1,) + (1,) * (len(extent) - axis_at - 1))

    factor_of = one(*cuts[0])
    for cut in cuts[1:]:
        factor_of = factor_of * one(*cut)
    return factor_of


def centred(stream_key, dims, spread, bound, shards=(), kind=jnp.bfloat16):
    values = jax.random.normal(stream_key, dims, jnp.float32) * spread
    if len(shards) > 0:
        values = steps_of(stream_key, dims, shards, -0.22, 0.18) * values
    return jnp.clip(values, min=-bound, max=bound).astype(kind)


def setup_inputs(seed: int = 0, part: int = 0) -> dict:
    arg_keys = jax.random.split(jax.random.key(seed), 11)
    own_keys = jax.random.split(jax.random.fold_in(arg_keys[10], part), 11)
    x_tiles = centred(own_keys[0], (TILES, S, S, C), 1.0, 6.0, ((0, 16),))
    h_tiles = centred(own_keys[1], (TILES, S, S, C), 1.0, 6.0, ((0, 16),))
    grad_out = centred(own_keys[2], (TILES, S, S, C), 1.0, 6.0, ((0, 16),))
    w_gate = centred(arg_keys[3], (18 * C, 2 * C), (18 * C) ** -0.5, 0.09375)
    b_gate = centred(arg_keys[4], (2 * C,), 1.0, 3.0, (), jnp.float32)
    w_cand = centred(arg_keys[5], (18 * C, C), (18 * C) ** -0.5, 0.09375)
    b_cand = centred(arg_keys[6], (C,), 1.0, 3.0, (), jnp.float32)
    partner_edge = draw_partner_edge(jax.random.fold_in(arg_keys[10], 71), part)
    edge_flip = draw_edge_flip(jax.random.fold_in(arg_keys[10], 71), part)
    tile_slot = draw_tile_slot(jax.random.fold_in(arg_keys[10], 71), part)
    return dict(x_tiles=x_tiles, h_tiles=h_tiles, grad_out=grad_out, w_gate=w_gate, b_gate=b_gate, w_cand=w_cand, b_cand=b_cand, partner_edge=partner_edge, edge_flip=edge_flip, tile_slot=tile_slot)


def edge_strips(stack):
    return jnp.stack([stack[:, 0], stack[:, :, -1], stack[:, -1], stack[:, :, 0]], axis=1)


def routing(partner_edge, edge_flip, tile_slot):
    tile_count = tile_slot.shape[0]
    holder = jnp.zeros((tile_count,), jnp.int32).at[tile_slot].set(jnp.arange(tile_count, dtype=jnp.int32))
    partners = partner_edge[holder]
    target = tile_slot[partners // 4] * 4 + partners % 4
    return target.astype(jnp.int32), edge_flip[holder]


def deliver(strip_all, target, flipped):
    flat_strips = strip_all.reshape((-1,) + strip_all.shape[2:])
    picked = flat_strips[target.reshape(-1)].reshape(strip_all.shape)
    return jnp.where(flipped[:, :, None, None] == 1, picked[:, :, ::-1], picked)


def framed(stack, arrived):
    padded = jnp.pad(stack, ((0, 0), (1, 1), (1, 1), (0, 0)))
    padded = padded.at[:, 0, 1:-1].set(arrived[:, 0])
    padded = padded.at[:, 1:-1, -1].set(arrived[:, 1])
    padded = padded.at[:, -1, 1:-1].set(arrived[:, 2])
    padded = padded.at[:, 1:-1, 0].set(arrived[:, 3])
    return padded


def patches_of(padded):
    tile_side = padded.shape[1] - 2
    columns = [padded[:, row_tap:row_tap + tile_side, col_tap:col_tap + tile_side] for row_tap in range(3) for col_tap in range(3)]
    return jnp.concatenate(columns, axis=-1).reshape(-1, 9 * padded.shape[-1])


def unpatch(dpatch, tile_count, tile_side, channels):
    dpatch = dpatch.reshape(tile_count, tile_side, tile_side, 9, channels)
    result = jnp.zeros((tile_count, tile_side + 2, tile_side + 2, channels), jnp.float32)
    for row_tap in range(3):
        for col_tap in range(3):
            result = result.at[:, row_tap:row_tap + tile_side, col_tap:col_tap + tile_side].add(dpatch[:, :, :, row_tap * 3 + col_tap])
    return result


def rim_of(padded):
    return jnp.stack([padded[:, 0, 1:-1], padded[:, 1:-1, -1], padded[:, -1, 1:-1], padded[:, 1:-1, 0]], axis=1)


def settle(padded, arrived):
    interior = padded[:, 1:-1, 1:-1]
    interior = interior.at[:, 0].add(arrived[:, 0])
    interior = interior.at[:, :, -1].add(arrived[:, 1])
    interior = interior.at[:, -1].add(arrived[:, 2])
    interior = interior.at[:, :, 0].add(arrived[:, 3])
    return interior


def reference(x_tiles, h_tiles, grad_out, w_gate, b_gate, w_cand, b_cand, partner_edge, edge_flip, tile_slot):
    tile_count = x_tiles.shape[0]
    tile_side = x_tiles.shape[1]
    channels = x_tiles.shape[3]
    target, flipped = routing(partner_edge, edge_flip, tile_slot)
    joined = jnp.concatenate([x_tiles, h_tiles], axis=-1)
    patch_gate = patches_of(framed(joined, deliver(edge_strips(joined), target, flipped)))
    gate_act = jax.nn.sigmoid(jnp.dot(patch_gate, w_gate, preferred_element_type=jnp.float32) + b_gate)
    update_gate = gate_act[:, :channels]
    reset_gate = gate_act[:, channels:]
    h_flat = h_tiles.reshape(-1, channels).astype(jnp.float32)
    reset_h = (reset_gate * h_flat).astype(jnp.bfloat16)
    mixed = jnp.concatenate([x_tiles, reset_h.reshape(tile_count, tile_side, tile_side, channels)], axis=-1)
    patch_cand = patches_of(framed(mixed, deliver(edge_strips(mixed), target, flipped)))
    candidate = jnp.tanh(jnp.dot(patch_cand, w_cand, preferred_element_type=jnp.float32) + b_cand)
    grad_flat = grad_out.reshape(-1, channels).astype(jnp.float32)
    d_update = grad_flat * (candidate - h_flat)
    d_cand_pre = (grad_flat * update_gate * (1.0 - candidate * candidate)).astype(jnp.bfloat16)
    grad_w_cand = jnp.dot(patch_cand.T, d_cand_pre, preferred_element_type=jnp.float32)
    grid_cand = unpatch(jnp.dot(d_cand_pre, w_cand.T, preferred_element_type=jnp.float32), tile_count, tile_side, 2 * channels)
    back_cand = settle(grid_cand, deliver(rim_of(grid_cand), target, flipped))
    d_rh = back_cand[..., channels:].reshape(-1, channels)
    d_gate_pre = jnp.concatenate([d_update * update_gate * (1.0 - update_gate), d_rh * h_flat * reset_gate * (1.0 - reset_gate)], axis=-1).astype(jnp.bfloat16)
    grad_w_gate = jnp.dot(patch_gate.T, d_gate_pre, preferred_element_type=jnp.float32)
    grid_gate = unpatch(jnp.dot(d_gate_pre, w_gate.T, preferred_element_type=jnp.float32), tile_count, tile_side, 2 * channels)
    back_gate = settle(grid_gate, deliver(rim_of(grid_gate), target, flipped))
    grad_x = (back_cand[..., :channels] + back_gate[..., :channels]).astype(jnp.bfloat16)
    direct = (grad_flat * (1.0 - update_gate) + d_rh * reset_gate).reshape(tile_count, tile_side, tile_side, channels)
    grad_h = (direct + back_gate[..., channels:]).astype(jnp.bfloat16)
    return grad_x, grad_h, grad_w_gate, grad_w_cand
```

```python
import functools

import jax
import jax.numpy as jnp
import numpy as np
from jax import lax
from jax.experimental import pallas as pl
from jax.experimental.pallas import tpu as pltpu
from jax.sharding import PartitionSpec as P

BF = jnp.bfloat16
F32 = jnp.float32


def dot(a, b):
    return jnp.dot(a, b, preferred_element_type=F32)


def dot_nt(a, b):
    return lax.dot_general(a, b, (((1,), (1,)), ((), ())), preferred_element_type=F32)


def dot_tn(a, b):
    return lax.dot_general(a, b, (((0,), (0,)), ((), ())), preferred_element_type=F32)


def call(body, outs, *args, flops=0, smem=(), mib=24):
    vmem = pl.BlockSpec(memory_space=pltpu.VMEM)
    in_specs = [pl.BlockSpec(memory_space=pltpu.SMEM) if i in smem else vmem for i in range(len(args))]
    size = sum(a.size * a.dtype.itemsize for a in args)
    size += sum(int(np.prod(s)) * jnp.dtype(d).itemsize for s, d in outs)
    return pl.pallas_call(
        body,
        out_shape=[jax.ShapeDtypeStruct(s, d) for s, d in outs],
        in_specs=in_specs,
        out_specs=[vmem] * len(outs),
        compiler_params=pltpu.CompilerParams(vmem_limit_bytes=mib * 2**20),
        cost_estimate=pl.CostEstimate(flops=int(flops), bytes_accessed=int(size), transcendentals=0),
    )(*args)


def frame_matrices(side):
    cells = side * side
    out = np.zeros((3, (side + 2) * side, cells + 4 * side), np.float32)
    for b in range(3):
        for r in range(side + 2):
            for j in range(side):
                c = j + b
                inner_r, inner_c = 1 <= r <= side, 1 <= c <= side
                if inner_r and inner_c:
                    src = (r - 1) * side + c - 1
                elif inner_c:
                    src = cells + (0 if r == 0 else 2) * side + c - 1
                elif inner_r:
                    src = cells + (3 if c == 0 else 1) * side + r - 1
                else:
                    continue
                out[b, r * side + j, src] = 1
    return out


def choose(index, values):
    out = jnp.full(index.shape, values[0], jnp.int32)
    for k in range(1, 4):
        out = jnp.where(index == k, values[k], out)
    return out


def edge_cell(edge, i, side):
    last = side - 1
    return jnp.where(
        edge == 0, i, jnp.where(edge == 1, i * side + last, jnp.where(edge == 2, last * side + i, i * side))
    )


def route_kernel(side, tiles, partner, flip, slot, x, h, send_next, send_prev, sel, place, turn, rim_sel):
    me = lax.axis_index("tile")
    after = jnp.where(me == tiles - 1, 0, me + 1)
    holder = lax.fori_loop(0, tiles, lambda t, a: a + jnp.where(slot[t] == me, t, 0), jnp.int32(0))
    q, fl, up = [], [], []
    for e in range(4):
        p = partner[holder, e]
        q.append(p & 3)
        fl.append(flip[holder, e])
        up.append((slot[p >> 2] == after).astype(jnp.int32))
    out_at, in_at = [], []
    for e in range(4):
        before = sum([jnp.where(up[o] == up[e], 1, 0) for o in range(e)], jnp.int32(0))
        lower = sum(
            [jnp.where((up[o] == up[e]) & (q[o] < q[e]), 1, 0) for o in range(4) if o != e], jnp.int32(0)
        )
        out_at.append(before + 2 * (1 - up[e]))
        in_at.append(lower + 2 * up[e])
    send_edge = [sum(jnp.where(out_at[e] == k, e, 0) for e in range(4)) for k in range(4)]
    recv_edge = [sum(jnp.where(in_at[e] == k, e, 0) for e in range(4)) for k in range(4)]
    recv_flip = [sum(jnp.where(in_at[e] == k, fl[e], 0) for e in range(4)) for k in range(4)]
    cells, rim = side * side, 4 * side

    def parts(shape, dim):
        at = lax.broadcasted_iota(jnp.int32, shape, dim)
        return at // side, at % side

    def one_hot(shape, dim, where_to):
        hit = lax.broadcasted_iota(jnp.int32, shape, dim) == where_to
        return jnp.where(hit, 1.0, 0.0).astype(BF)

    k, i = parts((rim, cells), 0)
    chosen = one_hot((rim, cells), 1, edge_cell(choose(k, send_edge), i, side))
    sel[...] = chosen
    for n, u in enumerate((x, h)):
        c = u.shape[1]
        picked = dot(chosen, u[...]).astype(BF)
        send_next[:, n * c : (n + 1) * c] = picked[: rim // 2]
        send_prev[:, n * c : (n + 1) * c] = picked[rim // 2 :]
    k, i = parts((cells, rim), 1)
    i = jnp.where(choose(k, recv_flip) == 1, side - 1 - i, i)
    place[...] = one_hot((cells, rim), 0, edge_cell(choose(k, recv_edge), i, side))
    k, i = parts((rim, rim), 1)
    i = jnp.where(choose(k, recv_flip) == 1, side - 1 - i, i)
    turn[...] = one_hot((rim, rim), 0, choose(k, recv_edge) * side + i)
    width = 2 * side + 2 * cells
    k, i = parts((rim, width), 0)
    e = choose(k, send_edge)
    at = jnp.where(
        e == 0,
        i,
        jnp.where(
            e == 2, side + i, jnp.where(e == 3, 2 * side + i * side, 2 * side + cells + i * side + side - 1)
        ),
    )
    rim_sel[...] = one_hot((rim, width), 1, at)


def frames(side, tile, strips, m0, m2, f):
    whole = jnp.concatenate([tile, strips], axis=0)
    f[0] = dot(m0[...], whole).astype(BF)
    f[1, :side] = strips[:side]
    f[1, side : side + side * side] = tile
    f[1, side + side * side :] = strips[2 * side : 3 * side]
    f[2] = dot(m2[...], whole).astype(BF)
    return whole


def conv(side, f, w, lo, hi):
    cells = side * side
    cols = [f[b, a * side : a * side + cells, :] for a in range(3) for b in range(3)]
    rows = [w[t, lo:hi, :] for t in range(9)]
    return dot(jnp.concatenate(cols, axis=1), jnp.concatenate(rows, axis=0))


def gate_kernel(side, x, h, rp, rn, turn, m0, m2, w, bias, sel, gate, rh, s_next, s_prev, f, whole):
    c = x.shape[1]
    rim = 4 * side
    strips = dot(turn[...], jnp.concatenate([rp[...], rn[...]], axis=0)).astype(BF)
    tile = jnp.concatenate([x[...], h[...]], axis=1)
    whole[...] = frames(side, tile, strips, m0, m2, f)
    act = jax.nn.sigmoid(conv(side, f, w, 0, 2 * c) + bias[...])
    gate[...] = act
    reset_h = (act[:, c:] * h[...].astype(F32)).astype(BF)
    rh[...] = reset_h
    picked = dot(sel[...], reset_h).astype(BF)
    s_next[...] = picked[: rim // 2]
    s_prev[...] = picked[rim // 2 :]


def cand_x_kernel(side, f, w, bias, out):
    c = w.shape[2]
    cells = side * side
    cols = [f[b, a * side : a * side + cells, :c] for a in range(3) for b in range(3)]
    rows = [w[t, :c, :] for t in range(9)]
    out[...] = dot(jnp.concatenate(cols, axis=1), jnp.concatenate(rows, axis=0)) + bias[...]


def cand_kernel(side, acc, rh, rp, rn, turn, m0, m2, w, gate, h, g, d, whole, f):
    c = rh.shape[1]
    strips = dot(turn[...], jnp.concatenate([rp[...], rn[...]], axis=0)).astype(BF)
    whole[...] = frames(side, rh[...], strips, m0, m2, f)
    candidate = jnp.tanh(acc[...] + conv(side, f, w, c, 2 * c))
    update = gate[:, :c]
    grad = g[...].astype(F32)
    d[:, :c] = (grad * update * (1.0 - candidate * candidate)).astype(BF)
    d[:, c:] = (grad * (candidate - h[...].astype(F32)) * update * (1.0 - update)).astype(BF)


def spread(side, acc, d, w, lo, hi, col_lo, col_hi, fresh):
    cells = side * side
    if fresh:
        acc[...] = jnp.zeros_like(acc)
    for a in range(3):
        for b in range(3):
            rows = slice(a * side, a * side + cells)
            acc[b, rows, :] += dot_nt(d, w[a * 3 + b, lo:hi, col_lo:col_hi])


def gather_frame(side, acc):
    cells, c = side * side, acc.shape[2]
    rows = (side + 2) * side
    col = lax.broadcasted_iota(jnp.int32, (rows, c), 0) % side
    left, right = acc[0], acc[2]
    total = acc[1]
    total += jnp.where(col == side - 1, 0.0, pltpu.roll(left, rows - 1, 0))
    total += jnp.where(col == 0, 0.0, pltpu.roll(right, 1, 0))
    rim = jnp.concatenate(
        [total[:side], total[side + cells :], left[side : side + cells], right[side : side + cells]], axis=0
    ).astype(BF)
    return total[side : side + cells], rim


def back_rh_kernel(side, d, w, rim_sel, inner, s_next, s_prev, acc):
    c = w.shape[2]
    rim = 4 * side
    spread(side, acc, d[:, :c], w, c, 2 * c, 0, c, True)
    own, edge = gather_frame(side, acc)
    inner[...] = own
    picked = dot(rim_sel[...], edge).astype(BF)
    s_next[...] = picked[: rim // 2]
    s_prev[...] = picked[rim // 2 :]


def back_early_kernel(side, d, wc, wg, acc):
    c = wc.shape[2]
    cells = side * side
    acc[...] = jnp.zeros_like(acc)
    for a in range(3):
        for b in range(3):
            rows = slice(a * side, a * side + cells)
            t = a * 3 + b
            acc[b, rows, :c] += dot_nt(d[:, :c], wc[t, :c, :]) + dot_nt(d[:, c:], wg[t, :c, :c])
            acc[b, rows, c:] += dot_nt(d[:, c:], wg[t, c:, :c])


def reset_kernel(side, inner, rp, rn, place, gate, h, g, d, direct):
    c = h.shape[1]
    d_rh = inner[...] + dot(place[...], jnp.concatenate([rp[...], rn[...]], axis=0))
    update, reset = gate[:, :c], gate[:, c:]
    d[...] = (d_rh * h[...].astype(F32) * reset * (1.0 - reset)).astype(BF)
    direct[...] = g[...].astype(F32) * (1.0 - update) + d_rh * reset


def back_gate_kernel(side, early, d, w, direct, rim_sel, inner, s_next, s_prev, acc):
    c = d.shape[1]
    rim = 4 * side
    acc[...] = early[...]
    spread(side, acc, d[...], w, 0, 2 * c, c, 2 * c, False)
    own, edge = gather_frame(side, acc)
    inner[:, :c] = own[:, :c]
    inner[:, c:] = own[:, c:] + direct[...]
    picked = dot(rim_sel[...], edge).astype(BF)
    s_next[...] = picked[: rim // 2]
    s_prev[...] = picked[rim // 2 :]


def final_kernel(inner, rp, rn, place, gx, gh):
    c = gx.shape[1]
    total = inner[...] + dot(place[...], jnp.concatenate([rp[...], rn[...]], axis=0))
    gx[...] = total[:, :c].astype(BF)
    gh[...] = total[:, c:].astype(BF)


def shards(
    x_tiles, h_tiles, grad_out, w_gate, b_gate, w_cand, b_cand, partner_edge, edge_flip, tile_slot
):
    side, c = x_tiles.shape[1], x_tiles.shape[3]
    tiles = lax.axis_size("tile")
    cells, rim = side * side, 4 * side
    half, band = rim // 2, (side + 2) * side
    x, h, g = (u.reshape(cells, c) for u in (x_tiles, h_tiles, grad_out))
    wg, wc = w_gate.reshape(9, 2 * c, 2 * c), w_cand.reshape(9, 2 * c, c)
    bg, bc = b_gate.reshape(1, 2 * c), b_cand.reshape(1, c)
    m = frame_matrices(side)
    m0, m2 = jnp.asarray(m[0], BF), jnp.asarray(m[2], BF)
    up = [(i, (i + 1) % tiles) for i in range(tiles)]
    down = [(j, i) for i, j in up]

    def exchange(s_next, s_prev):
        return lax.ppermute(s_next, "tile", up), lax.ppermute(s_prev, "tile", down)

    unit = 2 * cells * 9 * c * c
    with jax.named_scope("route"):
        s1n, s1p, sel, place, turn, rim_sel = call(
            functools.partial(route_kernel, side, tiles),
            [
                ((half, 2 * c), BF),
                ((half, 2 * c), BF),
                ((rim, cells), BF),
                ((cells, rim), BF),
                ((rim, rim), BF),
                ((rim, 2 * side + 2 * cells), BF),
            ],
            partner_edge, edge_flip, tile_slot, x, h, smem=(0, 1, 2),
        )
    r1p, r1n = exchange(s1n, s1p)
    with jax.named_scope("gate"):
        gate, rh, s2n, s2p, f, whole = call(
            functools.partial(gate_kernel, side),
            [
                ((cells, 2 * c), F32),
                ((cells, c), BF),
                ((half, c), BF),
                ((half, c), BF),
                ((3, band, 2 * c), BF),
                ((cells + rim, 2 * c), BF),
            ],
            x, h, r1p, r1n, turn, m0, m2, wg, bg, sel, flops=4 * unit,
        )
    r2p, r2n = exchange(s2n, s2p)
    with jax.named_scope("cand_x"):
        (acc_x,) = call(functools.partial(cand_x_kernel, side), [((cells, c), F32)], f, wc, bc, flops=unit)
    with jax.named_scope("cand"):
        d_cu, whole_rh, f_rh = call(
            functools.partial(cand_kernel, side),
            [((cells, 2 * c), BF), ((cells + rim, c), BF), ((3, band, c), BF)],
            acc_x, rh, r2p, r2n, turn, m0, m2, wc, gate, h, g, flops=unit,
        )
    with jax.named_scope("back_rh"):
        inner_rh, s3n, s3p, _ = call(
            functools.partial(back_rh_kernel, side),
            [((cells, c), F32), ((half, c), BF), ((half, c), BF), ((3, band, c), F32)],
            d_cu, wc, rim_sel, flops=unit,
        )
    r3p, r3n = exchange(s3n, s3p)
    with jax.named_scope("back_early"):
        (early,) = call(
            functools.partial(back_early_kernel, side), [((3, band, 2 * c), F32)], d_cu, wc, wg, flops=3 * unit
        )
    with jax.named_scope("reset"):
        d_r, direct = call(
            functools.partial(reset_kernel, side),
            [((cells, c), BF), ((cells, c), F32)],
            inner_rh, r3p, r3n, place, gate, h, g,
        )
    with jax.named_scope("back_gate"):
        inner, s4n, s4p, _ = call(
            functools.partial(back_gate_kernel, side),
            [((cells, 2 * c), F32), ((half, 2 * c), BF), ((half, 2 * c), BF), ((3, band, 2 * c), F32)],
            early, d_r, wg, direct, rim_sel, flops=2 * unit,
        )
    r4p, r4n = exchange(s4n, s4p)

    with jax.named_scope("weights"):
        def patch(u):
            return jnp.concatenate([u[b, a * side : a * side + cells] for a in range(3) for b in range(3)], axis=1)

        f_c = jnp.concatenate([f[:, :, :c], f_rh], axis=2)
        gwc = dot_tn(patch(f_c), d_cu[:, :c]).astype(BF)
        gwu = dot_tn(patch(f), d_cu[:, c:]).astype(BF)
        gwr = dot_tn(patch(f), d_r).astype(BF)
        first = lax.psum_scatter(
            jnp.concatenate([gwc, gwu], axis=1), "tile", scatter_dimension=0, tiled=True
        ).astype(F32)
        second = lax.psum_scatter(gwr, "tile", scatter_dimension=0, tiled=True).astype(F32)
        grad_w_cand = first[:, :c]
        grad_w_gate = jnp.concatenate([first[:, c:], second], axis=1)

    with jax.named_scope("final"):
        gx, gh = call(final_kernel, [((cells, c), BF), ((cells, c), BF)], inner, r4p, r4n, place)
    shape = (1, side, side, c)
    return gx.reshape(shape), gh.reshape(shape), grad_w_gate, grad_w_cand


def solution(mesh):
    tile = P(("grp", "tile"), None, None, None)
    rows = P(("grp", "tile"), None)
    return jax.shard_map(
        shards,
        mesh=mesh,
        in_specs=(tile, tile, tile) + (P(),) * 7,
        out_specs=(tile, tile, rows, rows),
        check_vma=False,
    )
```

```python
import functools

import jax
import jax.numpy as jnp
import numpy as np
from jax import lax
from jax.experimental import pallas as pl
from jax.experimental.pallas import tpu as pltpu
from jax.sharding import PartitionSpec as P

BF = jnp.bfloat16
F32 = jnp.float32


def dot(a, b):
    return jnp.dot(a, b, preferred_element_type=F32)


def dot_nt(a, b):
    return lax.dot_general(a, b, (((1,), (1,)), ((), ())), preferred_element_type=F32)


def dot_tn(a, b):
    return lax.dot_general(a, b, (((0,), (0,)), ((), ())), preferred_element_type=F32)


def call(body, outs, *args, flops=0, smem=(), mib=24, scratch=()):
    vmem = pl.BlockSpec(memory_space=pltpu.VMEM)
    in_specs = [pl.BlockSpec(memory_space=pltpu.SMEM) if i in smem else vmem for i in range(len(args))]
    size = sum(a.size * a.dtype.itemsize for a in args)
    size += sum(int(np.prod(s)) * jnp.dtype(d).itemsize for s, d in outs)
    return pl.pallas_call(
        body,
        out_shape=[jax.ShapeDtypeStruct(s, d) for s, d in outs],
        in_specs=in_specs,
        out_specs=[vmem] * len(outs),
        scratch_shapes=[pltpu.VMEM(s, d) for s, d in scratch],
        compiler_params=pltpu.CompilerParams(vmem_limit_bytes=mib * 2**20),
        cost_estimate=pl.CostEstimate(flops=int(flops), bytes_accessed=int(size), transcendentals=0),
    )(*args)


def frame_matrices(side):
    cells = side * side
    out = np.zeros((3, (side + 2) * side, cells + 4 * side), np.float32)
    for b in range(3):
        for r in range(side + 2):
            for j in range(side):
                c = j + b
                inner_r, inner_c = 1 <= r <= side, 1 <= c <= side
                if inner_r and inner_c:
                    src = (r - 1) * side + c - 1
                elif inner_c:
                    src = cells + (0 if r == 0 else 2) * side + c - 1
                elif inner_r:
                    src = cells + (3 if c == 0 else 1) * side + r - 1
                else:
                    continue
                out[b, r * side + j, src] = 1
    return out


def tap_matrices(side):
    m, cells = frame_matrices(side), side * side
    taps = [m[b, a * side : a * side + cells].T for a in range(3) for b in range(3)]
    return np.stack(taps)


def choose(index, values):
    out = jnp.full(index.shape, values[0], jnp.int32)
    for k in range(1, 4):
        out = jnp.where(index == k, values[k], out)
    return out


def edge_cell(edge, i, side):
    last = side - 1
    return jnp.where(
        edge == 0, i, jnp.where(edge == 1, i * side + last, jnp.where(edge == 2, last * side + i, i * side))
    )


def route_kernel(side, tiles, partner, flip, slot, x, h, xh, send_next, send_prev, sel, place, turn, rim_sel):
    me = lax.axis_index("tile")
    after = jnp.where(me == tiles - 1, 0, me + 1)
    holder = lax.fori_loop(0, tiles, lambda t, a: a + jnp.where(slot[t] == me, t, 0), jnp.int32(0))
    q, fl, up = [], [], []
    for e in range(4):
        p = partner[holder, e]
        q.append(p & 3)
        fl.append(flip[holder, e])
        up.append((slot[p >> 2] == after).astype(jnp.int32))
    out_at, in_at = [], []
    for e in range(4):
        before = sum([jnp.where(up[o] == up[e], 1, 0) for o in range(e)], jnp.int32(0))
        lower = sum(
            [jnp.where((up[o] == up[e]) & (q[o] < q[e]), 1, 0) for o in range(4) if o != e], jnp.int32(0)
        )
        out_at.append(before + 2 * (1 - up[e]))
        in_at.append(lower + 2 * up[e])
    send_edge = [sum(jnp.where(out_at[e] == k, e, 0) for e in range(4)) for k in range(4)]
    recv_edge = [sum(jnp.where(in_at[e] == k, e, 0) for e in range(4)) for k in range(4)]
    recv_flip = [sum(jnp.where(in_at[e] == k, fl[e], 0) for e in range(4)) for k in range(4)]
    cells, rim = side * side, 4 * side

    def parts(shape, dim):
        at = lax.broadcasted_iota(jnp.int32, shape, dim)
        return at // side, at % side

    def one_hot(shape, dim, where_to):
        hit = lax.broadcasted_iota(jnp.int32, shape, dim) == where_to
        return jnp.where(hit, 1.0, 0.0).astype(BF)

    k, i = parts((rim, cells), 0)
    chosen = one_hot((rim, cells), 1, edge_cell(choose(k, send_edge), i, side))
    sel[...] = chosen
    for n, u in enumerate((x, h)):
        c = u.shape[1]
        picked = dot(chosen, u[...]).astype(BF)
        send_next[:, n * c : (n + 1) * c] = picked[: rim // 2]
        send_prev[:, n * c : (n + 1) * c] = picked[rim // 2 :]
        xh[:, n * c : (n + 1) * c] = u[...]
    k, i = parts((cells, rim), 1)
    i = jnp.where(choose(k, recv_flip) == 1, side - 1 - i, i)
    place[...] = one_hot((cells, rim), 0, edge_cell(choose(k, recv_edge), i, side))
    k, i = parts((rim, rim), 1)
    i = jnp.where(choose(k, recv_flip) == 1, side - 1 - i, i)
    turn[...] = one_hot((rim, rim), 0, choose(k, recv_edge) * side + i)
    width = 2 * side + 2 * cells
    k, i = parts((rim, width), 0)
    e = choose(k, send_edge)
    at = jnp.where(
        e == 0,
        i,
        jnp.where(
            e == 2, side + i, jnp.where(e == 3, 2 * side + i * side, 2 * side + cells + i * side + side - 1)
        ),
    )
    rim_sel[...] = one_hot((rim, width), 1, at)


def frames(side, tile, strips, m0, m2, f):
    whole = jnp.concatenate([tile, strips], axis=0)
    f[0] = dot(m0[...], whole).astype(BF)
    f[1, :side] = strips[:side]
    f[1, side : side + side * side] = tile
    f[1, side + side * side :] = strips[2 * side : 3 * side]
    f[2] = dot(m2[...], whole).astype(BF)


def conv(side, f, w, lo, hi):
    cells = side * side
    cols = [f[b, a * side : a * side + cells, :] for a in range(3) for b in range(3)]
    rows = [w[t, lo:hi, :] for t in range(9)]
    return dot(jnp.concatenate(cols, axis=1), jnp.concatenate(rows, axis=0))


def gate_kernel(side, xh, rp, rn, turn, m0, m2, w, bias, sel, gate, pack, s_next, s_prev, f):
    c = xh.shape[1] // 2
    cells, rim = side * side, 4 * side
    strips = dot(turn[...], jnp.concatenate([rp[...], rn[...]], axis=0)).astype(BF)
    frames(side, xh[...], strips, m0, m2, f)
    act = jax.nn.sigmoid(conv(side, f, w, 0, 2 * c) + bias[...])
    gate[...] = act
    reset_h = (act[:, c:] * xh[:, c:].astype(F32)).astype(BF)
    pack[:cells] = reset_h
    pack[cells : cells + rim] = strips[:, :c]
    pack[cells + rim :] = strips[:, c:]
    picked = dot(sel[...], reset_h).astype(BF)
    s_next[...] = picked[: rim // 2]
    s_prev[...] = picked[rim // 2 :]


def cand_x_kernel(side, f, w, bias, out):
    c = w.shape[2]
    cells = side * side
    cols = [f[b, a * side : a * side + cells, :c] for a in range(3) for b in range(3)]
    rows = [w[t, :c, :] for t in range(9)]
    out[...] = dot(jnp.concatenate(cols, axis=1), jnp.concatenate(rows, axis=0)) + bias[...]


def cand_kernel(side, acc, pack, rp, rn, turn, m0, m2, w, gate, h, g, d, f):
    c = h.shape[1]
    cells, half = side * side, 2 * side
    strips = dot(turn[...], jnp.concatenate([rp[...], rn[...]], axis=0)).astype(BF)
    frames(side, pack[:cells], strips, m0, m2, f)
    d[cells:, :c] = strips[:half]
    d[cells:, c:] = strips[half:]
    candidate = jnp.tanh(acc[...] + conv(side, f, w, c, 2 * c))
    update = gate[:, :c]
    grad = g[...].astype(F32)
    d[:cells, :c] = (grad * update * (1.0 - candidate * candidate)).astype(BF)
    d[:cells, c:] = (grad * (candidate - h[...].astype(F32)) * update * (1.0 - update)).astype(BF)


def spread(side, acc, d, w, lo, hi, col_lo, col_hi, fresh):
    cells = side * side
    if fresh:
        acc[...] = jnp.zeros_like(acc)
    for a in range(3):
        for b in range(3):
            rows = slice(a * side, a * side + cells)
            acc[b, rows, :] += dot_nt(d, w[a * 3 + b, lo:hi, col_lo:col_hi])


def gather_frame(side, acc):
    cells, c = side * side, acc.shape[2]
    rows = (side + 2) * side
    col = lax.broadcasted_iota(jnp.int32, (rows, c), 0) % side
    left, right = acc[0], acc[2]
    total = acc[1]
    total += jnp.where(col == side - 1, 0.0, pltpu.roll(left, rows - 1, 0))
    total += jnp.where(col == 0, 0.0, pltpu.roll(right, 1, 0))
    rim = jnp.concatenate(
        [total[:side], total[side + cells :], left[side : side + cells], right[side : side + cells]], axis=0
    ).astype(BF)
    return total[side : side + cells], rim


def back_rh_kernel(side, d, w, rim_sel, inner, s_next, s_prev, acc):
    c = w.shape[2]
    rim = 4 * side
    spread(side, acc, d[: side * side, :c], w, c, 2 * c, 0, c, True)
    own, edge = gather_frame(side, acc)
    inner[...] = own
    picked = dot(rim_sel[...], edge).astype(BF)
    s_next[...] = picked[: rim // 2]
    s_prev[...] = picked[rim // 2 :]


def back_early_kernel(side, d, wc, wg, acc):
    c = wc.shape[2]
    cells = side * side
    acc[...] = jnp.zeros_like(acc)
    for a in range(3):
        for b in range(3):
            rows = slice(a * side, a * side + cells)
            t = a * 3 + b
            acc[b, rows, :c] += dot_nt(d[:cells, :c], wc[t, :c, :]) + dot_nt(d[:cells, c:], wg[t, :c, :c])
            acc[b, rows, c:] += dot_nt(d[:cells, c:], wg[t, c:, :c])


def reset_kernel(side, inner, rp, rn, place, gate, h, g, d, direct):
    c = h.shape[1]
    d_rh = inner[...] + dot(place[...], jnp.concatenate([rp[...], rn[...]], axis=0))
    update, reset = gate[:, :c], gate[:, c:]
    d[...] = (d_rh * h[...].astype(F32) * reset * (1.0 - reset)).astype(BF)
    direct[...] = g[...].astype(F32) * (1.0 - update) + d_rh * reset


def back_gate_kernel(side, early, d, w, direct, rim_sel, inner, s_next, s_prev, acc):
    c = d.shape[1]
    rim = 4 * side
    acc[...] = early[...]
    spread(side, acc, d[...], w, 0, 2 * c, c, 2 * c, False)
    own, edge = gather_frame(side, acc)
    inner[:, :c] = own[:, :c]
    inner[:, c:] = own[:, c:] + direct[...]
    picked = dot(rim_sel[...], edge).astype(BF)
    s_next[...] = picked[: rim // 2]
    s_prev[...] = picked[rim // 2 :]


def final_kernel(inner, rp, rn, place, gx, gh):
    c = gx.shape[1]
    total = inner[...] + dot(place[...], jnp.concatenate([rp[...], rn[...]], axis=0))
    gx[...] = total[:, :c].astype(BF)
    gh[...] = total[:, c:].astype(BF)


def lhs_kernel(side, rows, tiles, cand, *refs):
    xh, packs, ds = refs[:4], refs[4:8], refs[8:12]
    taps, out, src = refs[-3:]
    cells, rim, half = side * side, 4 * side, 2 * side
    c = packs[0].shape[1]
    per_tap = 2 * c // 128
    for n in range(4):
        lanes = slice(n * 128, (n + 1) * 128)
        for k in range(per_tap):
            at = slice(k * 128, (k + 1) * 128)
            if k < per_tap // 2 or not cand:
                src[k, :cells, lanes] = xh[n][:, at]
                col = slice(at.start % c, at.start % c + 128)
                first = cells if at.start < c else cells + rim
                src[k, cells:, lanes] = packs[n][first : first + rim, col]
            else:
                col = slice(at.start - c, at.start - c + 128)
                src[k, :cells, lanes] = packs[n][:cells, col]
                src[k, cells : cells + half, lanes] = ds[n][cells:, col]
                src[k, cells + half :, lanes] = ds[n][cells:, at]
    me = lax.axis_index("tile")
    for t in range(out.shape[0]):
        target = me ^ (8 * (t // 2) + t % 2)
        for n in range(out.shape[1] // 128):
            block = jnp.minimum(target * rows // 128 + n, 9 * per_tap - 1)
            part = dot_tn(src[block % per_tap], taps[block // per_tap]).astype(BF)
            for k in range(4):
                out[t, n * 128 : (n + 1) * 128, k * cells : (k + 1) * cells] = part[k * 128 : (k + 1) * 128]


def weight_kernel(side, rows, n_lhs, *refs):
    lhs, ds, (keep, send, acc) = refs[:n_lhs], refs[n_lhs : n_lhs + 4], refs[-3:]
    cells = side * side
    me = lax.axis_index("tile")
    c = ds[0].shape[1] // n_lhs
    right = jnp.concatenate([d[:cells] for d in ds], axis=0)
    for t in range(lhs[0].shape[0]):
        target = me ^ (8 * (t // 2) + t % 2)
        first = pl.multiple_of(target * rows % 128, 8)
        for k in range(n_lhs):
            acc[t % 2, :, k * c : (k + 1) * c] = dot(lhs[k][t], right[:, k * c : (k + 1) * c])
        part = acc[t % 2, pl.ds(first, rows), :]
        if t % 2 == 0:
            keep[t // 2] = part
        else:
            send[t // 2] = part.astype(BF)


def pair_kernel(keep, got, own, far):
    own[...] = keep[0] + got[0].astype(F32)
    for m in range(1, keep.shape[0]):
        far[m - 1] = (keep[m] + got[m].astype(F32)).astype(BF)


def sum_kernel(n_far, *refs):
    first, second, (cand, gate) = refs[: n_far + 1], refs[n_far + 1 : -2], refs[-2:]
    c = cand.shape[1]
    total = first[0][...]
    for r in first[1:]:
        total += r[...].astype(F32)
    cand[...] = total[:, :c]
    gate[:, :c] = total[:, c:]
    total = second[0][...]
    for r in second[1:]:
        total += r[...].astype(F32)
    gate[:, c:] = total


def shards(
    x_tiles, h_tiles, grad_out, w_gate, b_gate, w_cand, b_cand, partner_edge, edge_flip, tile_slot
):
    side, c = x_tiles.shape[1], x_tiles.shape[3]
    tiles = lax.axis_size("tile")
    cells, rim = side * side, 4 * side
    half, band = rim // 2, (side + 2) * side
    rows = 18 * c // tiles
    groups = tiles // 8
    blocks = max((rows * j + rows - 1) // 128 - rows * j // 128 + 1 for j in range(tiles)) * 128
    x, h, g = (u.reshape(cells, c) for u in (x_tiles, h_tiles, grad_out))
    wg, wc = w_gate.reshape(9, 2 * c, 2 * c), w_cand.reshape(9, 2 * c, c)
    bg, bc = b_gate.reshape(1, 2 * c), b_cand.reshape(1, c)
    m = frame_matrices(side)
    m0, m2 = jnp.asarray(m[0], BF), jnp.asarray(m[2], BF)
    taps = jnp.asarray(tap_matrices(side), BF)
    up = [(i, (i + 1) % tiles) for i in range(tiles)]
    down = [(j, i) for i, j in up]

    def exchange(s_next, s_prev):
        return lax.ppermute(s_next, "tile", up), lax.ppermute(s_prev, "tile", down)

    def swap(u, k):
        return lax.ppermute(u, "tile", [(i, i ^ k) for i in range(tiles)])

    def near(u):
        return [u] + [swap(u, k) for k in (2, 4, 6)]

    unit = 2 * cells * 9 * c * c
    with jax.named_scope("route"):
        xh, s1n, s1p, sel, place, turn, rim_sel = call(
            functools.partial(route_kernel, side, tiles),
            [
                ((cells, 2 * c), BF),
                ((half, 2 * c), BF),
                ((half, 2 * c), BF),
                ((rim, cells), BF),
                ((cells, rim), BF),
                ((rim, rim), BF),
                ((rim, 2 * side + 2 * cells), BF),
            ],
            partner_edge, edge_flip, tile_slot, x, h, smem=(0, 1, 2),
        )
    r1p, r1n = exchange(s1n, s1p)
    xh_near = near(xh)
    with jax.named_scope("gate"):
        gate, pack, s2n, s2p, f = call(
            functools.partial(gate_kernel, side),
            [
                ((cells, 2 * c), F32),
                ((cells + 2 * rim, c), BF),
                ((half, c), BF),
                ((half, c), BF),
                ((3, band, 2 * c), BF),
            ],
            xh, r1p, r1n, turn, m0, m2, wg, bg, sel, flops=4 * unit,
        )
    r2p, r2n = exchange(s2n, s2p)
    pack_near = near(pack)
    with jax.named_scope("cand_x"):
        (acc_x,) = call(functools.partial(cand_x_kernel, side), [((cells, c), F32)], f, wc, bc, flops=unit)
    with jax.named_scope("cand"):
        d_cu, _ = call(
            functools.partial(cand_kernel, side),
            [((cells + half, 2 * c), BF), ((3, band, c), BF)],
            acc_x, pack, r2p, r2n, turn, m0, m2, wc, gate, h, g, flops=unit,
        )
    d_near = near(d_cu)
    with jax.named_scope("back_rh"):
        inner_rh, s3n, s3p, _ = call(
            functools.partial(back_rh_kernel, side),
            [((cells, c), F32), ((half, c), BF), ((half, c), BF), ((3, band, c), F32)],
            d_cu, wc, rim_sel, flops=unit,
        )
    r3p, r3n = exchange(s3n, s3p)
    with jax.named_scope("back_early"):
        (early,) = call(
            functools.partial(back_early_kernel, side), [((3, band, 2 * c), F32)], d_cu, wc, wg, flops=3 * unit
        )
    with jax.named_scope("reset"):
        d_r, direct = call(
            functools.partial(reset_kernel, side),
            [((cells, c), BF), ((cells, c), F32)],
            inner_rh, r3p, r3n, place, gate, h, g,
        )
    r_near = near(d_r)
    with jax.named_scope("back_gate"):
        inner, s4n, s4p, _ = call(
            functools.partial(back_gate_kernel, side),
            [((cells, 2 * c), F32), ((half, 2 * c), BF), ((half, 2 * c), BF), ((3, band, 2 * c), F32)],
            early, d_r, wg, direct, rim_sel, flops=2 * unit,
        )
    r4p, r4n = exchange(s4n, s4p)

    def lhs_of(cand, *args):
        return call(
            functools.partial(lhs_kernel, side, rows, tiles, cand),
            [((2 * groups, blocks, 4 * cells), BF)],
            *args, taps,
            flops=2 * 2 * groups * blocks * 4 * cells * (cells + rim),
            scratch=[((2 * c // 128, cells + rim, 512), BF)],
        )[0]

    def partial_sums(lhs, ds):
        n = len(lhs)
        keep, send = call(
            functools.partial(weight_kernel, side, rows, n),
            [((groups, rows, n * c), F32), ((groups, rows, n * c), BF)],
            *lhs, *ds,
            flops=2 * 2 * groups * blocks * 4 * cells * n * c,
            scratch=[((2, blocks, n * c), F32)],
        )
        own, far = call(
            pair_kernel, [((rows, n * c), F32), ((groups - 1, rows, n * c), BF)], keep, swap(send, 1)
        )
        return [own] + [swap(far[k - 1], 8 * k) for k in range(1, groups)]

    with jax.named_scope("lhs_gate"):
        lhs_gate = lhs_of(False, *xh_near, *pack_near)
    with jax.named_scope("lhs_cand"):
        lhs_cand = lhs_of(True, *xh_near, *pack_near, *d_near)
    with jax.named_scope("weights_first"):
        first = partial_sums([lhs_cand, lhs_gate], d_near)
    with jax.named_scope("weights_second"):
        second = partial_sums([lhs_gate], r_near)
    with jax.named_scope("weights_sum"):
        grad_w_cand, grad_w_gate = call(
            functools.partial(sum_kernel, groups - 1),
            [((rows, c), F32), ((rows, 2 * c), F32)],
            *first, *second,
        )
    with jax.named_scope("final"):
        gx, gh = call(final_kernel, [((cells, c), BF), ((cells, c), BF)], inner, r4p, r4n, place)
    shape = (1, side, side, c)
    return gx.reshape(shape), gh.reshape(shape), grad_w_gate, grad_w_cand


def solution(mesh):
    tile = P(("grp", "tile"), None, None, None)
    rows = P(("grp", "tile"), None)
    return jax.shard_map(
        shards,
        mesh=mesh,
        in_specs=(tile, tile, tile) + (P(),) * 7,
        out_specs=(tile, tile, rows, rows),
        check_vma=False,
    )
```

```python
import functools

import jax
import jax.numpy as jnp
import numpy as np
from jax import lax
from jax.experimental import pallas as pl
from jax.experimental.pallas import tpu as pltpu
from jax.sharding import PartitionSpec as P

BF = jnp.bfloat16
F32 = jnp.float32


def dot(a, b):
    return jnp.dot(a, b, preferred_element_type=F32)


def dot_nt(a, b):
    return lax.dot_general(a, b, (((1,), (1,)), ((), ())), preferred_element_type=F32)


def dot_tn(a, b):
    return lax.dot_general(a, b, (((0,), (0,)), ((), ())), preferred_element_type=F32)


def call(body, outs, *args, mib=24, scratch=(), hbm=(), pin=True, cost=0):
    vmem = pl.BlockSpec(memory_space=pltpu.VMEM)
    far = pl.BlockSpec(memory_space=pltpu.HBM)
    in_specs = [far if i in hbm else vmem for i in range(len(args))]
    args = [pltpu.with_memory_space_constraint(a, pltpu.HBM) if i in hbm else a for i, a in enumerate(args)]
    return pl.pallas_call(
        body,
        out_shape=[pltpu.VMEM(s, d) if pin else jax.ShapeDtypeStruct(s, d) for s, d in outs],
        in_specs=in_specs,
        out_specs=[vmem] * len(outs),
        scratch_shapes=list(scratch),
        compiler_params=pltpu.CompilerParams(vmem_limit_bytes=mib * 2**20),
        cost_estimate=pl.CostEstimate(flops=cost * 10**9, bytes_accessed=0, transcendentals=0),
    )(*args)


def frame_matrices(side):
    cells = side * side
    out = np.zeros((3, (side + 2) * side, cells + 4 * side), np.float32)
    for b in range(3):
        for r in range(side + 2):
            for j in range(side):
                c = j + b
                inner_r, inner_c = 1 <= r <= side, 1 <= c <= side
                if inner_r and inner_c:
                    src = (r - 1) * side + c - 1
                elif inner_c:
                    src = cells + (0 if r == 0 else 2) * side + c - 1
                elif inner_r:
                    src = cells + (3 if c == 0 else 1) * side + r - 1
                else:
                    continue
                out[b, r * side + j, src] = 1
    return out


def tap_matrices(side):
    m, cells = frame_matrices(side), side * side
    taps = [m[b, a * side : a * side + cells].T for a in range(3) for b in range(3)]
    return np.stack(taps)


def choose(index, values):
    out = jnp.full(index.shape, values[0], jnp.int32)
    for k in range(1, 4):
        out = jnp.where(index == k, values[k], out)
    return out


def edge_cell(edge, i, side):
    last = side - 1
    return jnp.where(
        edge == 0, i, jnp.where(edge == 1, i * side + last, jnp.where(edge == 2, last * side + i, i * side))
    )


def route_kernel(side, tiles, p_in, f_in, s_in, x, h, xh, s_first, s_second, sel, place, turn, rim_sel, partner, flip, slot, sems):
    c = x.shape[1]
    loads = [(p_in, partner), (f_in, flip), (s_in, slot), (x, xh.at[:, :c]), (h, xh.at[:, c:])]
    loads = [pltpu.make_async_copy(a, b, sems.at[n]) for n, (a, b) in enumerate(loads)]
    for copy in loads:
        copy.start()
    for copy in loads[:3]:
        copy.wait()
    me = lax.axis_index("tile")
    holder = lax.fori_loop(0, tiles, lambda t, a: a + jnp.where(slot[t] == me, t, 0), jnp.int32(0))
    q, fl, up = [], [], []
    for e in range(4):
        p = partner[e, holder]
        q.append(p & 3)
        fl.append(flip[e, holder])
        up.append((slot[p >> 2] == (me ^ 1)).astype(jnp.int32))
    out_at, in_at = [], []
    for e in range(4):
        before = sum([jnp.where(up[o] == up[e], 1, 0) for o in range(e)], jnp.int32(0))
        lower = sum(
            [jnp.where((up[o] == up[e]) & (q[o] < q[e]), 1, 0) for o in range(4) if o != e], jnp.int32(0)
        )
        out_at.append(before + 2 * (1 - up[e]))
        in_at.append(lower + 2 * (1 - up[e]))
    send_edge = [sum(jnp.where(out_at[e] == k, e, 0) for e in range(4)) for k in range(4)]
    recv_edge = [sum(jnp.where(in_at[e] == k, e, 0) for e in range(4)) for k in range(4)]
    recv_flip = [sum(jnp.where(in_at[e] == k, fl[e], 0) for e in range(4)) for k in range(4)]
    cells, rim = side * side, 4 * side

    def parts(shape, dim):
        at = lax.broadcasted_iota(jnp.int32, shape, dim)
        return at // side, at % side

    def one_hot(shape, dim, where_to):
        hit = lax.broadcasted_iota(jnp.int32, shape, dim) == where_to
        return jnp.where(hit, 1.0, 0.0).astype(BF)

    k, i = parts((rim, cells), 0)
    chosen = one_hot((rim, cells), 1, edge_cell(choose(k, send_edge), i, side))
    sel[...] = chosen
    for copy in loads[3:]:
        copy.wait()
    picked = dot(chosen, xh[...]).astype(BF)
    s_first[...] = picked[: rim // 2]
    s_second[...] = picked[rim // 2 :]
    k, i = parts((cells, rim), 1)
    i = jnp.where(choose(k, recv_flip) == 1, side - 1 - i, i)
    place[...] = one_hot((cells, rim), 0, edge_cell(choose(k, recv_edge), i, side))
    k, i = parts((rim, rim), 1)
    i = jnp.where(choose(k, recv_flip) == 1, side - 1 - i, i)
    turn[...] = one_hot((rim, rim), 0, choose(k, recv_edge) * side + i)
    width = 2 * side + 2 * cells
    k, i = parts((rim, width), 0)
    e = choose(k, send_edge)
    at = jnp.where(
        e == 0,
        i,
        jnp.where(
            e == 2, side + i, jnp.where(e == 3, 2 * side + i * side, 2 * side + cells + i * side + side - 1)
        ),
    )
    rim_sel[...] = one_hot((rim, width), 1, at)


def frames(side, tile, strips, m0, m2, f):
    whole = jnp.concatenate([tile, strips], axis=0)
    f[0] = dot(m0[...], whole).astype(BF)
    f[1, :side] = strips[:side]
    f[1, side : side + side * side] = tile
    f[1, side + side * side :] = strips[2 * side : 3 * side]
    f[2] = dot(m2[...], whole).astype(BF)


def conv(side, f, w, lo, hi, col_lo=0, col_hi=None):
    cells = side * side
    cols = [f[b, a * side : a * side + cells, :] for a in range(3) for b in range(3)]
    rows = [w[t, lo:hi, col_lo:col_hi] for t in range(9)]
    return dot(jnp.concatenate(cols, axis=1), jnp.concatenate(rows, axis=0))


def gate_kernel(side, xh, rp, rn, turn, m0, m2, w, bias, sel, gate, rh, pack, s_next, s_prev, f):
    c = xh.shape[1] // 2
    cells, rim = side * side, 4 * side
    strips = dot(turn[...], jnp.concatenate([rp[...], rn[...]], axis=0)).astype(BF)
    frames(side, xh[...], strips, m0, m2, f)
    act = jax.nn.sigmoid(conv(side, f, w, 0, 2 * c) + bias[...])
    gate[...] = act
    reset_h = (act[:, c:] * xh[:, c:].astype(F32)).astype(BF)
    rh[...] = reset_h
    pack[:cells] = xh[:, c:]
    pack[cells : cells + rim] = strips[:, :c]
    pack[cells + rim :] = strips[:, c:]
    picked = dot(sel[...], reset_h).astype(BF)
    s_next[...] = picked[: rim // 2]
    s_prev[...] = picked[rim // 2 :]


def load_kernel(n, *refs):
    sems = refs[-1]
    copies = [pltpu.make_async_copy(refs[k], refs[n + k], sems.at[k]) for k in range(n)]
    for copy in copies:
        copy.start()
    for copy in copies:
        copy.wait()


def cand_x_kernel(side, f, w, bias, out):
    c = w.shape[2]
    cells = side * side
    cols = [f[b, a * side : a * side + cells, :c] for a in range(3) for b in range(3)]
    rows = [w[t, :c, :] for t in range(9)]
    out[...] = dot(jnp.concatenate(cols, axis=1), jnp.concatenate(rows, axis=0)) + bias[...]


def cand_kernel(side, acc, rh, rp, rn, turn, m0, m2, w, gate, h, g, d, f):
    c = g.shape[1]
    cells = side * side
    strips = dot(turn[...], jnp.concatenate([rp[...], rn[...]], axis=0)).astype(BF)
    frames(side, rh[...], strips, m0, m2, f)
    d[2 * cells :] = strips
    candidate = jnp.tanh(acc[...] + conv(side, f, w, c, 2 * c))
    update = gate[:, :c]
    grad = g[...].astype(F32)
    d[:cells] = (grad * update * (1.0 - candidate * candidate)).astype(BF)
    d[cells : 2 * cells] = (grad * (candidate - h[:, c:].astype(F32)) * update * (1.0 - update)).astype(BF)


def spread(side, acc, d, w, lo, hi, col_lo, col_hi, fresh):
    cells = side * side
    if fresh:
        acc[...] = jnp.zeros_like(acc)
    for a in range(3):
        for b in range(3):
            rows = slice(a * side, a * side + cells)
            acc[b, rows, :] += dot_nt(d, w[a * 3 + b, lo:hi, col_lo:col_hi])


def gather_frame(side, acc):
    cells, c = side * side, acc.shape[2]
    rows = (side + 2) * side
    col = lax.broadcasted_iota(jnp.int32, (rows, c), 0) % side
    left, right = acc[0], acc[2]
    total = acc[1]
    total += jnp.where(col == side - 1, 0.0, pltpu.roll(left, rows - 1, 0))
    total += jnp.where(col == 0, 0.0, pltpu.roll(right, 1, 0))
    rim = jnp.concatenate(
        [total[:side], total[side + cells :], left[side : side + cells], right[side : side + cells]], axis=0
    ).astype(BF)
    return total[side : side + cells], rim


def back_rh_kernel(side, d, w, rim_sel, inner, s_next, s_prev, acc):
    c = w.shape[2]
    rim = 4 * side
    spread(side, acc, d[: side * side], w, c, 2 * c, 0, c, True)
    own, edge = gather_frame(side, acc)
    inner[...] = own
    picked = dot(rim_sel[...], edge).astype(BF)
    s_next[...] = picked[: rim // 2]
    s_prev[...] = picked[rim // 2 :]


def back_early_kernel(side, d, wc, wg, acc):
    c = wc.shape[2]
    cells = side * side
    acc[...] = jnp.zeros_like(acc)
    for a in range(3):
        for b in range(3):
            rows = slice(a * side, a * side + cells)
            t = a * 3 + b
            acc[b, rows, :c] += dot_nt(d[:cells], wc[t, :c, :]) + dot_nt(d[cells : 2 * cells], wg[t, :c, :c])
            acc[b, rows, c:] += dot_nt(d[cells : 2 * cells], wg[t, c:, :c])


def reset_kernel(side, inner, rp, rn, place, gate, h, g, d_cu, d, direct):
    c = g.shape[1]
    d_rh = inner[...] + dot(place[...], jnp.concatenate([rp[...], rn[...]], axis=0))
    update, reset = gate[:, :c], gate[:, c:]
    cells = side * side
    d[: 2 * cells] = d_cu[: 2 * cells]
    d[3 * cells :] = d_cu[2 * cells :]
    d[2 * cells : 3 * cells] = (d_rh * h[:, c:].astype(F32) * reset * (1.0 - reset)).astype(BF)
    direct[...] = g[...].astype(F32) * (1.0 - update) + d_rh * reset


def back_gate_kernel(side, early, d, w, direct, rim_sel, inner, s_next, s_prev, acc):
    c = d.shape[1]
    rim = 4 * side
    acc[...] = early[...]
    cells = side * side
    spread(side, acc, d[2 * cells : 3 * cells], w, 0, 2 * c, c, 2 * c, False)
    own, edge = gather_frame(side, acc)
    inner[:, :c] = own[:, :c]
    inner[:, c:] = own[:, c:] + direct[...]
    picked = dot(rim_sel[...], edge).astype(BF)
    s_next[...] = picked[: rim // 2]
    s_prev[...] = picked[rim // 2 :]


def final_kernel(inner, rp, rn, place, gx, gh):
    c = gx.shape[1]
    total = inner[...] + dot(place[...], jnp.concatenate([rp[...], rn[...]], axis=0))
    gx[...] = total[:, :c].astype(BF)
    gh[...] = total[:, c:].astype(BF)


def near_reset_kernel(side, *refs):
    x, packs, (m0, m2, w, bias, out, f) = refs[1:4], refs[5:8], refs[8:]
    cells, rim, c = side * side, 4 * side, out.shape[2]
    for n in range(3):
        h = packs[n][:cells]
        tile = jnp.concatenate([x[n][...], h], axis=1)
        strips = jnp.concatenate([packs[n][cells : cells + rim], packs[n][cells + rim :]], axis=1)
        frames(side, tile, strips, m0, m2, f)
        reset = jax.nn.sigmoid(conv(side, f, w, 0, 2 * c, c, 2 * c) + bias[:, c:])
        out[n] = (reset * h.astype(F32)).astype(BF)


def lhs_kernel(side, rows, tiles, cand, *refs):
    x, packs, more = refs[:4], refs[4:8], refs[8:-3]
    me = lax.axis_index("tile")
    taps, out, src = refs[-3:]
    cells, rim = side * side, 4 * side
    c = packs[0].shape[1]
    per_tap = 2 * c // 128
    for n in range(4):
        lanes = slice(n * 128, (n + 1) * 128)
        for k in range(per_tap):
            at = slice(k * 128, (k + 1) * 128)
            col = slice(at.start % c, at.start % c + 128)
            if at.start < c:
                src[k, :cells, lanes] = x[n][:, col]
                src[k, cells:, lanes] = packs[n][cells : cells + rim, col]
            elif cand:
                rh, rh_near, ds = more[0], more[1], more[2:]
                src[k, :cells, lanes] = rh[:, col] if n == 0 else rh_near[n - 1, :, col]
                src[k, cells:, lanes] = ds[n][3 * cells :, col]
            else:
                src[k, :cells, lanes] = packs[n][:cells, col]
                src[k, cells:, lanes] = packs[n][cells + rim :, col]
    for t in range(out.shape[0]):
        target = me ^ (8 * (t // 2) + t % 2)
        for n in range(out.shape[1] // 128):
            block = jnp.minimum(target * rows // 128 + n, 9 * per_tap - 1)
            part = dot_tn(src[block % per_tap], taps[block // per_tap]).astype(BF)
            for k in range(4):
                out[t, n * 128 : (n + 1) * 128, k * cells : (k + 1) * cells] = part[k * 128 : (k + 1) * 128]


def weight_kernel(side, rows, parts, lhs, d0, d1, d2, d3, keep, *refs):
    sends, acc = refs[:-1], refs[-1]
    cells = side * side
    me = lax.axis_index("tile")
    width = sends[0].shape[2]
    right = [jnp.concatenate([d[k * cells : (k + 1) * cells] for k in parts], axis=1) for d in (d0, d1, d2, d3)]
    right = jnp.concatenate(right, axis=0)
    for t in range(lhs.shape[0]):
        target = me ^ (8 * (t // 2) + t % 2)
        first = pl.multiple_of(target * rows % 128, 8)
        acc[t % 2] = dot(lhs[t], right)
        part = acc[t % 2, pl.ds(first, rows), :]
        if t % 2 == 0:
            keep[t // 2] = part
        else:
            for k, send in enumerate(sends):
                send[t // 2] = part[:, k * width : (k + 1) * width].astype(BF)


def pair_kernel(keep, *refs):
    got, (own, far) = refs[:-2], refs[-2:]
    width = got[0].shape[2]
    for k, part in enumerate(got):
        at = slice(k * width, (k + 1) * width)
        own[:, at] = keep[0, :, at] + part[0].astype(F32)
        for m in range(1, keep.shape[0]):
            far[m - 1, :, at] = (keep[m, :, at] + part[m].astype(F32)).astype(BF)


def sum_kernel(own, *refs):
    total = own[...]
    for r in refs[:-1]:
        total += r[...].astype(F32)
    refs[-1][...] = total


def shards(
    x_tiles, h_tiles, grad_out, w_gate, b_gate, w_cand, b_cand, partner_edge, edge_flip, tile_slot
):
    side, c = x_tiles.shape[1], x_tiles.shape[3]
    tiles = lax.axis_size("tile")
    cells, rim = side * side, 4 * side
    half, band = rim // 2, (side + 2) * side
    rows = 18 * c // tiles
    groups = tiles // 8
    blocks = max((rows * j + rows - 1) // 128 - rows * j // 128 + 1 for j in range(tiles)) * 128
    x, h, g = (u.reshape(cells, c) for u in (x_tiles, h_tiles, grad_out))
    wg, wc = w_gate.reshape(9, 2 * c, 2 * c), w_cand.reshape(9, 2 * c, c)
    bg, bc = b_gate.reshape(1, 2 * c), b_cand.reshape(1, c)
    m = frame_matrices(side)
    m0, m2 = jnp.asarray(m[0], BF), jnp.asarray(m[2], BF)
    taps = jnp.asarray(tap_matrices(side), BF)
    cross = [(i, (i + 1) % tiles if i % 2 else (i - 1) % tiles) for i in range(tiles)]
    ran = []

    def run(name, body, outs, *args, **options):
        if ran:
            args = (after(args[0], ran[-1]),) + args[1:]
        with jax.named_scope(name):
            results = call(body, outs, *args, **options)
        ran.append(results[0])
        return results

    def load(name, *args):
        n = len(args)
        return run(
            name, functools.partial(load_kernel, n), [(a.shape, a.dtype) for a in args], *args,
            hbm=range(n), scratch=[pltpu.SemaphoreType.DMA((n,))],
        )

    def after(u, *others):
        return lax.optimization_barrier((u,) + others)[0]

    def swap(u, k):
        return lax.ppermute(u, "tile", [(i, i ^ k) for i in range(tiles)])

    def exchange(s_first, s_second):
        return swap(s_first, 1), lax.ppermute(s_second, "tile", cross)

    def near(u):
        return [u] + [swap(u, k) for k in (2, 4, 6)]

    def lhs_of(name, cand, *args):
        return run(
            name, functools.partial(lhs_kernel, side, rows, tiles, cand),
            [((2 * groups, blocks, 4 * cells), BF)],
            *args, taps_v,
            scratch=[pltpu.VMEM((2 * c // 128, cells + rim, 512), BF)],
        )[0]

    def products(name, parts, lhs, ds):
        n = len(parts)
        keep, *sends = run(
            name, functools.partial(weight_kernel, side, rows, parts),
            [((groups, rows, n * c), F32)] + [((groups, rows, n * c // 2), BF)] * 2,
            lhs, *ds,
            scratch=[pltpu.VMEM((2, blocks, n * c), F32)],
        )
        return keep, [swap(u, 1) for u in sends]

    def pair(name, keep, got):
        n = keep.shape[2]
        own, far = run(name, pair_kernel, [((rows, n), F32), ((groups - 1, rows, n), BF)], keep, *got)
        return [own] + [swap(far[k - 1], 8 * k) for k in range(1, groups)]

    xh, s1n, s1p, sel, place, turn, rim_sel = run(
        "route", functools.partial(route_kernel, side, tiles),
        [
            ((cells, 2 * c), BF),
            ((half, 2 * c), BF),
            ((half, 2 * c), BF),
            ((rim, cells), BF),
            ((cells, rim), BF),
            ((rim, rim), BF),
            ((rim, 2 * side + 2 * cells), BF),
        ],
        partner_edge.T, edge_flip.T, tile_slot, x, h,
        hbm=(0, 1, 2, 3, 4),
        scratch=[
            pltpu.SMEM((4, tiles), jnp.int32),
            pltpu.SMEM((4, tiles), jnp.int32),
            pltpu.SMEM((tiles,), jnp.int32),
            pltpu.SemaphoreType.DMA((5,)),
        ],
    )
    r1p, r1n = exchange(s1n, s1p)
    wg_v, m0, m2, bg_v = load("load_gate", wg, m0, m2, bg)
    x_near = near(after(x, bg_v))
    gate, rh, pack, s2n, s2p, f = run(
        "gate", functools.partial(gate_kernel, side),
        [
            ((cells, 2 * c), F32),
            ((cells, c), BF),
            ((cells + 2 * rim, c), BF),
            ((half, c), BF),
            ((half, c), BF),
            ((3, band, 2 * c), BF),
        ],
        xh, r1p, r1n, turn, m0, m2, wg_v, bg_v, sel, cost=5,
    )
    r2p, r2n = exchange(s2n, s2p)
    wc_v, bc_v, g_v = load("load_cand", wc, bc, g)
    pack_near = near(after(pack, *x_near))
    (acc_x,) = run("cand_x", functools.partial(cand_x_kernel, side), [((cells, c), F32)], f, wc_v, bc_v)
    d_cu, _ = run(
        "cand", functools.partial(cand_kernel, side),
        [((2 * cells + rim, c), BF), ((3, band, c), BF)],
        acc_x, rh, r2p, r2n, turn, m0, m2, wc_v, gate, xh, g_v, cost=3,
    )
    inner_rh, s3n, s3p, _ = run(
        "back_rh", functools.partial(back_rh_kernel, side),
        [((cells, c), F32), ((half, c), BF), ((half, c), BF), ((3, band, c), F32)],
        d_cu, wc_v, rim_sel,
    )
    r3p, r3n = exchange(s3n, s3p)
    (early,) = run(
        "back_early", functools.partial(back_early_kernel, side), [((3, band, 2 * c), F32)], d_cu, wc_v, wg_v
    )
    (taps_v,) = load("load_taps", taps)
    d, direct = run(
        "reset", functools.partial(reset_kernel, side),
        [((3 * cells + rim, c), BF), ((cells, c), F32)],
        inner_rh, r3p, r3n, place, gate, xh, g_v, d_cu,
    )
    d_near = near(after(d, *pack_near))
    lhs_gate = lhs_of("lhs_gate", False, *x_near, *pack_near)
    (rh_near,) = run(
        "near_reset", functools.partial(near_reset_kernel, side), [((3, cells, c), BF)],
        *x_near, *pack_near, m0, m2, wg_v, bg_v,
        scratch=[pltpu.VMEM((3, band, 2 * c), BF)],
    )
    inner, s4n, s4p, _ = run(
        "back_gate", functools.partial(back_gate_kernel, side),
        [((cells, 2 * c), F32), ((half, 2 * c), BF), ((half, 2 * c), BF), ((3, band, 2 * c), F32)],
        early, d, wg_v, direct, rim_sel,
    )
    r4p, r4n = exchange(s4n, s4p)
    keep_g, got_g = products("weights_gate", (1, 2), lhs_gate, d_near)
    gx, gh = run(
        "final", final_kernel, [((cells, c), BF), ((cells, c), BF)], inner, r4p, r4n, place, pin=False, cost=5
    )
    parts_g = pair("pair_gate", keep_g, got_g)
    lhs_cand = lhs_of("lhs_cand", True, *x_near, *pack_near, rh, rh_near, *d_near)
    keep_c, got_c = products("weights_cand", (0,), lhs_cand, d_near)
    parts_c = pair("pair_cand", keep_c, got_c)
    (grad_w_gate,) = run("sum_gate", sum_kernel, [((rows, 2 * c), F32)], *parts_g, pin=False, cost=2)
    (grad_w_cand,) = run("sum_cand", sum_kernel, [((rows, c), F32)], *parts_c, pin=False)
    shape = (1, side, side, c)
    return gx.reshape(shape), gh.reshape(shape), grad_w_gate, grad_w_cand


def solution(mesh):
    tile = P(("grp", "tile"), None, None, None)
    rows = P(("grp", "tile"), None)
    return jax.shard_map(
        shards,
        mesh=mesh,
        in_specs=(tile, tile, tile) + (P(),) * 7,
        out_specs=(tile, tile, rows, rows),
        check_vma=False,
    )
```

```python
import functools

import jax
import jax.numpy as jnp
import numpy as np
from jax import lax
from jax.experimental import pallas as pl
from jax.experimental.pallas import tpu as pltpu
from jax.sharding import PartitionSpec as P

BF = jnp.bfloat16
F32 = jnp.float32


def dot(a, b):
    return jnp.dot(a, b, preferred_element_type=F32)


def dot_nt(a, b):
    return lax.dot_general(a, b, (((1,), (1,)), ((), ())), preferred_element_type=F32)


def dot_tn(a, b):
    return lax.dot_general(a, b, (((0,), (0,)), ((), ())), preferred_element_type=F32)


def call(body, outs, *args, mib=24, scratch=(), hbm=(), pin=True, cost=0, aliases=None):
    vmem = pl.BlockSpec(memory_space=pltpu.VMEM)
    far = pl.BlockSpec(memory_space=pltpu.HBM)
    in_specs = [far if i in hbm else vmem for i in range(len(args))]
    args = [pltpu.with_memory_space_constraint(a, pltpu.HBM) if i in hbm else a for i, a in enumerate(args)]
    return pl.pallas_call(
        body,
        out_shape=[pltpu.VMEM(s, d) if pin else jax.ShapeDtypeStruct(s, d) for s, d in outs],
        in_specs=in_specs,
        out_specs=[vmem] * len(outs),
        scratch_shapes=list(scratch),
        input_output_aliases=aliases or {},
        compiler_params=pltpu.CompilerParams(vmem_limit_bytes=mib * 2**20),
        cost_estimate=pl.CostEstimate(flops=cost * 10**9, bytes_accessed=0, transcendentals=0),
    )(*args)


def frame_matrices(side):
    cells = side * side
    out = np.zeros((3, (side + 2) * side, cells + 4 * side), np.float32)
    for b in range(3):
        for r in range(side + 2):
            for j in range(side):
                c = j + b
                inner_r, inner_c = 1 <= r <= side, 1 <= c <= side
                if inner_r and inner_c:
                    src = (r - 1) * side + c - 1
                elif inner_c:
                    src = cells + (0 if r == 0 else 2) * side + c - 1
                elif inner_r:
                    src = cells + (3 if c == 0 else 1) * side + r - 1
                else:
                    continue
                out[b, r * side + j, src] = 1
    return out


def tap_matrices(side):
    m, cells = frame_matrices(side), side * side
    taps = [m[b, a * side : a * side + cells].T for a in range(3) for b in range(3)]
    return np.stack(taps)


def choose(index, values):
    out = jnp.full(index.shape, values[0], jnp.int32)
    for k in range(1, 4):
        out = jnp.where(index == k, values[k], out)
    return out


def edge_cell(edge, i, side):
    last = side - 1
    return jnp.where(
        edge == 0, i, jnp.where(edge == 1, i * side + last, jnp.where(edge == 2, last * side + i, i * side))
    )


def route_kernel(side, tiles, p_in, f_in, s_in, x, h, xh, s_first, s_second, sel, place, turn, rim_sel, partner, flip, slot, sems):
    c = x.shape[1]
    loads = [(p_in, partner), (f_in, flip), (s_in, slot), (x, xh.at[:, :c]), (h, xh.at[:, c:])]
    loads = [pltpu.make_async_copy(a, b, sems.at[n]) for n, (a, b) in enumerate(loads)]
    for copy in loads:
        copy.start()
    for copy in loads[:3]:
        copy.wait()
    me = lax.axis_index("tile")
    holder = lax.fori_loop(0, tiles, lambda t, a: a + jnp.where(slot[t] == me, t, 0), jnp.int32(0))
    q, fl, up = [], [], []
    for e in range(4):
        p = partner[e, holder]
        q.append(p & 3)
        fl.append(flip[e, holder])
        up.append((slot[p >> 2] == (me ^ 1)).astype(jnp.int32))
    out_at, in_at = [], []
    for e in range(4):
        before = sum([jnp.where(up[o] == up[e], 1, 0) for o in range(e)], jnp.int32(0))
        lower = sum(
            [jnp.where((up[o] == up[e]) & (q[o] < q[e]), 1, 0) for o in range(4) if o != e], jnp.int32(0)
        )
        out_at.append(before + 2 * (1 - up[e]))
        in_at.append(lower + 2 * (1 - up[e]))
    send_edge = [sum(jnp.where(out_at[e] == k, e, 0) for e in range(4)) for k in range(4)]
    recv_edge = [sum(jnp.where(in_at[e] == k, e, 0) for e in range(4)) for k in range(4)]
    recv_flip = [sum(jnp.where(in_at[e] == k, fl[e], 0) for e in range(4)) for k in range(4)]
    cells, rim = side * side, 4 * side

    def parts(shape, dim):
        at = lax.broadcasted_iota(jnp.int32, shape, dim)
        return at // side, at % side

    def one_hot(shape, dim, where_to):
        hit = lax.broadcasted_iota(jnp.int32, shape, dim) == where_to
        return jnp.where(hit, 1.0, 0.0).astype(BF)

    k, i = parts((rim, cells), 0)
    chosen = one_hot((rim, cells), 1, edge_cell(choose(k, send_edge), i, side))
    sel[...] = chosen
    for copy in loads[3:]:
        copy.wait()
    picked = dot(chosen, xh[...]).astype(BF)
    s_first[...] = picked[: rim // 2]
    s_second[...] = picked[rim // 2 :]
    k, i = parts((cells, rim), 1)
    i = jnp.where(choose(k, recv_flip) == 1, side - 1 - i, i)
    place[...] = one_hot((cells, rim), 0, edge_cell(choose(k, recv_edge), i, side))
    k, i = parts((rim, rim), 1)
    i = jnp.where(choose(k, recv_flip) == 1, side - 1 - i, i)
    turn[...] = one_hot((rim, rim), 0, choose(k, recv_edge) * side + i)
    width = 2 * side + 2 * cells
    k, i = parts((rim, width), 0)
    e = choose(k, send_edge)
    at = jnp.where(
        e == 0,
        i,
        jnp.where(
            e == 2, side + i, jnp.where(e == 3, 2 * side + i * side, 2 * side + cells + i * side + side - 1)
        ),
    )
    rim_sel[...] = one_hot((rim, width), 1, at)


def frames(side, tile, strips, m0, m2, f):
    whole = jnp.concatenate([tile, strips], axis=0)
    f[0] = dot(m0[...], whole).astype(BF)
    f[1, :side] = strips[:side]
    f[1, side : side + side * side] = tile
    f[1, side + side * side :] = strips[2 * side : 3 * side]
    f[2] = dot(m2[...], whole).astype(BF)


def conv(side, f, w, lo, hi, col_lo=0, col_hi=None):
    cells = side * side
    cols = [f[b, a * side : a * side + cells, :] for a in range(3) for b in range(3)]
    rows = [w[t, lo:hi, col_lo:col_hi] for t in range(9)]
    return dot(jnp.concatenate(cols, axis=1), jnp.concatenate(rows, axis=0))


def start_loads(pairs, sems):
    copies = [pltpu.make_async_copy(a, b, sems.at[k]) for k, (a, b) in enumerate(pairs)]
    for copy in copies:
        copy.start()
    return copies


def gate_kernel(
    side, xh, rp, rn, turn, m0, m2, w, bias, sel, wc_in, bc_in, g_in, gate, rh, pack, s_next, s_prev, f, wc, bc, g, sems
):
    copies = start_loads([(wc_in, wc), (bc_in, bc), (g_in, g)], sems)
    c = xh.shape[1] // 2
    cells, rim = side * side, 4 * side
    strips = dot(turn[...], jnp.concatenate([rp[...], rn[...]], axis=0)).astype(BF)
    frames(side, xh[...], strips, m0, m2, f)
    act = jax.nn.sigmoid(conv(side, f, w, 0, 2 * c) + bias[...])
    gate[...] = act
    reset_h = (act[:, c:] * xh[:, c:].astype(F32)).astype(BF)
    rh[...] = reset_h
    pack[:cells] = xh[:, c:]
    pack[cells : cells + rim] = strips[:, :c]
    pack[cells + rim :] = strips[:, c:]
    picked = dot(sel[...], reset_h).astype(BF)
    s_next[...] = picked[: rim // 2]
    s_prev[...] = picked[rim // 2 :]
    for copy in copies:
        copy.wait()


def load_kernel(n, *refs):
    for copy in start_loads([(refs[k], refs[n + k]) for k in range(n)], refs[-1]):
        copy.wait()


def cand_x_kernel(side, f, w, bias, out):
    c = w.shape[2]
    cells = side * side
    cols = [f[b, a * side : a * side + cells, :c] for a in range(3) for b in range(3)]
    rows = [w[t, :c, :] for t in range(9)]
    out[...] = dot(jnp.concatenate(cols, axis=1), jnp.concatenate(rows, axis=0)) + bias[...]


def cand_kernel(side, acc, rh, rp, rn, turn, m0, m2, w, gate, h, g, d, f):
    c = g.shape[1]
    cells = side * side
    strips = dot(turn[...], jnp.concatenate([rp[...], rn[...]], axis=0)).astype(BF)
    frames(side, rh[...], strips, m0, m2, f)
    d[2 * cells :] = strips
    candidate = jnp.tanh(acc[...] + conv(side, f, w, c, 2 * c))
    update = gate[:, :c]
    grad = g[...].astype(F32)
    d[:cells] = (grad * update * (1.0 - candidate * candidate)).astype(BF)
    d[cells : 2 * cells] = (grad * (candidate - h[:, c:].astype(F32)) * update * (1.0 - update)).astype(BF)


def spread(side, acc, d, w, lo, hi, col_lo, col_hi, fresh):
    cells = side * side
    if fresh:
        acc[...] = jnp.zeros_like(acc)
    for a in range(3):
        for b in range(3):
            rows = slice(a * side, a * side + cells)
            acc[b, rows, :] += dot_nt(d, w[a * 3 + b, lo:hi, col_lo:col_hi])


def gather_frame(side, acc):
    cells, c = side * side, acc.shape[2]
    rows = (side + 2) * side
    col = lax.broadcasted_iota(jnp.int32, (rows, c), 0) % side
    left, right = acc[0], acc[2]
    total = acc[1]
    total += jnp.where(col == side - 1, 0.0, pltpu.roll(left, rows - 1, 0))
    total += jnp.where(col == 0, 0.0, pltpu.roll(right, 1, 0))
    rim = jnp.concatenate(
        [total[:side], total[side + cells :], left[side : side + cells], right[side : side + cells]], axis=0
    ).astype(BF)
    return total[side : side + cells], rim


def back_rh_kernel(side, d, w, rim_sel, inner, s_next, s_prev, acc):
    c = w.shape[2]
    rim = 4 * side
    spread(side, acc, d[: side * side], w, c, 2 * c, 0, c, True)
    own, edge = gather_frame(side, acc)
    inner[...] = own
    picked = dot(rim_sel[...], edge).astype(BF)
    s_next[...] = picked[: rim // 2]
    s_prev[...] = picked[rim // 2 :]


def back_early_kernel(side, d, wc, wg, acc):
    c = wc.shape[2]
    cells = side * side
    acc[...] = jnp.zeros_like(acc)
    for a in range(3):
        for b in range(3):
            rows = slice(a * side, a * side + cells)
            t = a * 3 + b
            acc[b, rows, :c] += dot_nt(d[:cells], wc[t, :c, :]) + dot_nt(d[cells : 2 * cells], wg[t, :c, :c])
            acc[b, rows, c:] += dot_nt(d[cells : 2 * cells], wg[t, c:, :c])


def reset_kernel(side, inner, rp, rn, place, gate, h, g, d, direct):
    c = g.shape[1]
    d_rh = inner[...] + dot(place[...], jnp.concatenate([rp[...], rn[...]], axis=0))
    update, reset = gate[:, :c], gate[:, c:]
    d[...] = (d_rh * h[:, c:].astype(F32) * reset * (1.0 - reset)).astype(BF)
    direct[...] = g[...].astype(F32) * (1.0 - update) + d_rh * reset


def back_gate_kernel(side, early, d, w, direct, rim_sel, inner, s_next, s_prev, acc):
    c = d.shape[1]
    rim = 4 * side
    acc[...] = early[...]
    spread(side, acc, d[...], w, 0, 2 * c, c, 2 * c, False)
    own, edge = gather_frame(side, acc)
    inner[:, :c] = own[:, :c]
    inner[:, c:] = own[:, c:] + direct[...]
    picked = dot(rim_sel[...], edge).astype(BF)
    s_next[...] = picked[: rim // 2]
    s_prev[...] = picked[rim // 2 :]


def final_kernel(inner, rp, rn, place, gx, gh):
    c = gx.shape[1]
    total = inner[...] + dot(place[...], jnp.concatenate([rp[...], rn[...]], axis=0))
    gx[...] = total[:, :c].astype(BF)
    gh[...] = total[:, c:].astype(BF)


def near_reset_kernel(side, *refs):
    x, packs, (m0, m2, w, bias, taps_in, out, taps, f, sems) = refs[1:4], refs[5:8], refs[8:]
    (copy,) = start_loads([(taps_in, taps)], sems)
    cells, rim, c = side * side, 4 * side, out.shape[2]
    for n in range(3):
        tile = jnp.concatenate([x[n][...], packs[n][:cells]], axis=1)
        strips = jnp.concatenate([packs[n][cells : cells + rim], packs[n][cells + rim :]], axis=1)
        frames(side, tile, strips, m0, m2, f.at[n])
    cols = [
        jnp.concatenate([f[n, b, a * side : a * side + cells, :] for n in range(3)], axis=0)
        for a in range(3)
        for b in range(3)
    ]
    rows = [w[t, :, c:] for t in range(9)]
    reset = jax.nn.sigmoid(dot(jnp.concatenate(cols, axis=1), jnp.concatenate(rows, axis=0)) + bias[:, c:])
    for n in range(3):
        out[n] = (reset[n * cells : (n + 1) * cells] * packs[n][:cells].astype(F32)).astype(BF)
    copy.wait()


def lhs_kernel(side, rows, tiles, cand, *refs):
    x, packs, more = refs[:4], refs[4:8], refs[8:-4]
    me = lax.axis_index("tile")
    taps, out, src, turned = refs[-4:]
    cells, rim = side * side, 4 * side
    c = packs[0].shape[1]
    per_tap = 2 * c // 128
    for n in range(4):
        lanes = slice(n * 128, (n + 1) * 128)
        for k in range(per_tap):
            at = slice(k * 128, (k + 1) * 128)
            col = slice(at.start % c, at.start % c + 128)
            if at.start < c:
                src[k, :cells, lanes] = x[n][:, col]
                src[k, cells:, lanes] = packs[n][cells : cells + rim, col]
            elif cand:
                rh, rh_near, ds = more[0], more[1], more[2:]
                src[k, :cells, lanes] = rh[:, col] if n == 0 else rh_near[n - 1, :, col]
                src[k, cells:, lanes] = ds[n][2 * cells :, col]
            else:
                src[k, :cells, lanes] = packs[n][:cells, col]
                src[k, cells:, lanes] = packs[n][cells + rim :, col]
    for k in range(per_tap):
        turned[k] = src[k].T
    for t in range(out.shape[0]):
        target = me ^ (8 * (t // 2) + t % 2)
        for n in range(out.shape[1] // 128):
            block = jnp.minimum(target * rows // 128 + n, 9 * per_tap - 1)
            part = dot(turned[block % per_tap], taps[block // per_tap]).astype(BF)
            for k in range(4):
                out[t, n * 128 : (n + 1) * 128, k * cells : (k + 1) * cells] = part[k * 128 : (k + 1) * 128]


def weight_kernel(side, rows, parts, *refs):
    n = len(parts)
    lhs, ds, keep, sends, acc = refs[:n], refs[n : n + 4], refs[n + 4], refs[n + 5 : -1], refs[-1]
    cells = side * side
    c, width = ds[0].shape[1], sends[0].shape[2]
    me = lax.axis_index("tile")
    right = [jnp.concatenate([d[k * cells : (k + 1) * cells] for d in ds], axis=0) for k in parts]
    for t in range(lhs[0].shape[0]):
        target = me ^ (8 * (t // 2) + t % 2)
        first = pl.multiple_of(target * rows % 128, 8)
        for k in range(n):
            acc[k, t % 2] = dot(lhs[k][t], right[k])
            part = acc[k, t % 2, pl.ds(first, rows), :]
            if t % 2 == 0:
                keep[t // 2, :, k * c : (k + 1) * c] = part
            else:
                for j in range(c // width):
                    sends[k * (c // width) + j][t // 2] = part[:, j * width : (j + 1) * width].astype(BF)


def pair_kernel(keep, *refs):
    gots, (own, far) = refs[:-2], refs[-2:]
    c = gots[0].shape[2]
    for k, got in enumerate(gots):
        at = slice(k * c, (k + 1) * c)
        own[:, at] = keep[0, :, at] + got[0].astype(F32)
        for m in range(1, keep.shape[0]):
            far[m - 1, :, at] = (keep[m, :, at] + got[m].astype(F32)).astype(BF)


def sum_kernel(*refs):
    parts, (cand, update) = refs[:-2], refs[-2:]
    c = cand.shape[1]
    total = parts[0][...]
    for r in parts[1:]:
        total += r[...].astype(F32)
    cand[...] = total[:, :c]
    update[...] = total[:, c:]


def sum_reset_kernel(update, *refs):
    parts, gate = refs[:-1], refs[-1]
    c = update.shape[1]
    total = parts[0][...]
    for r in parts[1:]:
        total += r[...].astype(F32)
    gate[:, :c] = update[...]
    gate[:, c:] = total


def shards(
    x_tiles, h_tiles, grad_out, w_gate, b_gate, w_cand, b_cand, partner_edge, edge_flip, tile_slot
):
    side, c = x_tiles.shape[1], x_tiles.shape[3]
    tiles = lax.axis_size("tile")
    cells, rim = side * side, 4 * side
    half, band = rim // 2, (side + 2) * side
    rows = 18 * c // tiles
    groups = tiles // 8
    blocks = max((rows * j + rows - 1) // 128 - rows * j // 128 + 1 for j in range(tiles)) * 128
    x, h, g = (u.reshape(cells, c) for u in (x_tiles, h_tiles, grad_out))
    wg, wc = w_gate.reshape(9, 2 * c, 2 * c), w_cand.reshape(9, 2 * c, c)
    bg, bc = b_gate.reshape(1, 2 * c), b_cand.reshape(1, c)
    m = frame_matrices(side)
    m0, m2 = jnp.asarray(m[0], BF), jnp.asarray(m[2], BF)
    taps = jnp.asarray(tap_matrices(side), BF)
    cross = [(i, (i + 1) % tiles if i % 2 else (i - 1) % tiles) for i in range(tiles)]
    ran = []

    def run(name, body, outs, *args, **options):
        if ran:
            args = (after(args[0], ran[-1]),) + args[1:]
        with jax.named_scope(name):
            results = call(body, outs, *args, **options)
        ran.append(results[0])
        return results

    def load(name, *args):
        n = len(args)
        return run(
            name, functools.partial(load_kernel, n), [(a.shape, a.dtype) for a in args], *args,
            hbm=range(n), scratch=[pltpu.SemaphoreType.DMA((n,))],
        )

    def after(u, *others):
        return lax.optimization_barrier((u,) + others)[0]

    def swap(u, k):
        return lax.ppermute(u, "tile", [(i, i ^ k) for i in range(tiles)])

    def exchange(s_first, s_second):
        return swap(s_first, 1), lax.ppermute(s_second, "tile", cross)

    def near(u):
        return [u] + [swap(u, k) for k in (2, 4, 6)]

    def lhs_of(name, cand, *args, cost=0):
        return run(
            name, functools.partial(lhs_kernel, side, rows, tiles, cand),
            [((2 * groups, blocks, 4 * cells), BF)],
            *args, taps_v,
            scratch=[
                pltpu.VMEM((2 * c // 128, cells + rim, 512), BF),
                pltpu.VMEM((2 * c // 128, 512, cells + rim), BF),
            ],
            cost=cost,
        )[0]

    def products(name, parts, lhs, ds, cuts=1, cost=0):
        n = len(parts)
        keep, *sends = run(
            name, functools.partial(weight_kernel, side, rows, parts),
            [((groups, rows, n * c), F32)] + [((groups, rows, c // cuts), BF)] * (n * cuts),
            *lhs, *ds,
            scratch=[pltpu.VMEM((n, 2, blocks, c), F32)],
            cost=cost,
        )
        return keep, [swap(u, 1) for u in sends]

    def pair(name, keep, gots, cost=0):
        n = keep.shape[2]
        own, far = run(
            name, pair_kernel, [((rows, n), F32), ((groups - 1, rows, n), BF)], keep, *gots, cost=cost
        )
        return [own] + [swap(far[k - 1], 8 * k) for k in range(1, groups)]

    xh, s1n, s1p, sel, place, turn, rim_sel = run(
        "route", functools.partial(route_kernel, side, tiles),
        [
            ((cells, 2 * c), BF),
            ((half, 2 * c), BF),
            ((half, 2 * c), BF),
            ((rim, cells), BF),
            ((cells, rim), BF),
            ((rim, rim), BF),
            ((rim, 2 * side + 2 * cells), BF),
        ],
        partner_edge.T, edge_flip.T, tile_slot, x, h,
        hbm=(0, 1, 2, 3, 4),
        scratch=[
            pltpu.SMEM((4, tiles), jnp.int32),
            pltpu.SMEM((4, tiles), jnp.int32),
            pltpu.SMEM((tiles,), jnp.int32),
            pltpu.SemaphoreType.DMA((5,)),
        ],
    )
    r1p, r1n = exchange(s1n, s1p)
    x_near = near(x)
    wg_v, m0, m2, bg_v = load("load_gate", wg, m0, m2, bg)
    gate, rh, pack, s2n, s2p, f, wc_v, bc_v, g_v = run(
        "gate", functools.partial(gate_kernel, side),
        [
            ((cells, 2 * c), F32),
            ((cells, c), BF),
            ((cells + 2 * rim, c), BF),
            ((half, c), BF),
            ((half, c), BF),
            ((3, band, 2 * c), BF),
            (wc.shape, BF),
            (bc.shape, F32),
            (g.shape, BF),
        ],
        after(xh, *x_near), r1p, r1n, turn, m0, m2, wg_v, bg_v, sel, wc, bc, g,
        hbm=(9, 10, 11), scratch=[pltpu.SemaphoreType.DMA((3,))], cost=5,
    )
    r2p, r2n = exchange(s2n, s2p)
    pack_near = near(after(pack, *x_near))
    (acc_x,) = run("cand_x", functools.partial(cand_x_kernel, side), [((cells, c), F32)], f, wc_v, bc_v)
    d_cu, _ = run(
        "cand", functools.partial(cand_kernel, side),
        [((2 * cells + rim, c), BF), ((3, band, c), BF)],
        acc_x, rh, r2p, r2n, turn, m0, m2, wc_v, gate, xh, g_v, cost=3,
    )
    inner_rh, s3n, s3p, _ = run(
        "back_rh", functools.partial(back_rh_kernel, side),
        [((cells, c), F32), ((half, c), BF), ((half, c), BF), ((3, band, c), F32)],
        d_cu, wc_v, rim_sel,
    )
    r3p, r3n = exchange(s3n, s3p)
    d_near = near(after(d_cu, s3n, *pack_near))
    rh_near, taps_v = run(
        "near_reset", functools.partial(near_reset_kernel, side), [((3, cells, c), BF), (taps.shape, BF)],
        *x_near, *pack_near, m0, m2, wg_v, bg_v, taps,
        hbm=(12,),
        scratch=[pltpu.VMEM((3, 3, band, 2 * c), BF), pltpu.SemaphoreType.DMA((1,))],
    )
    lhs_gate = lhs_of("lhs_gate", False, *x_near, *pack_near, cost=5)
    d_r, direct = run(
        "reset", functools.partial(reset_kernel, side),
        [((cells, c), BF), ((cells, c), F32)],
        inner_rh, r3p, r3n, place, gate, xh, g_v,
    )
    r_near = near(d_r)
    lhs_cand = lhs_of("lhs_cand", True, *x_near, *pack_near, rh, rh_near, *d_near)
    keep_f, gots_f = products("weights_first", (0, 1), [lhs_cand, lhs_gate], d_near, cost=0)
    keep, gots = products("weights_reset", (0,), [lhs_gate], r_near, cuts=2, cost=4)
    parts = pair("pair_first", keep_f, gots_f, cost=0)
    parts_r = pair("pair_reset", keep, gots, cost=0)
    (early,) = run(
        "back_early", functools.partial(back_early_kernel, side), [((3, band, 2 * c), F32)], d_cu, wc_v, wg_v
    )
    inner, s4n, s4p, _ = run(
        "back_gate", functools.partial(back_gate_kernel, side),
        [((cells, 2 * c), F32), ((half, 2 * c), BF), ((half, 2 * c), BF), ((3, band, 2 * c), F32)],
        early, d_r, wg_v, direct, rim_sel, cost=0,
    )
    r4p, r4n = exchange(s4n, s4p)
    grad_w_cand, sum_u = run(
        "sum_first", sum_kernel, [((rows, c), F32), ((rows, c), F32)], *parts, pin=False, cost=2
    )
    gx, gh = run(
        "final", final_kernel, [((cells, c), BF), ((cells, c), BF)], inner, r4p, r4n, place, pin=False, cost=0
    )
    (grad_w_gate,) = run("sum_reset", sum_reset_kernel, [((rows, 2 * c), F32)], sum_u, *parts_r, pin=False)
    shape = (1, side, side, c)
    return gx.reshape(shape), gh.reshape(shape), grad_w_gate, grad_w_cand


def solution(mesh):
    tile = P(("grp", "tile"), None, None, None)
    rows = P(("grp", "tile"), None)
    return jax.shard_map(
        shards,
        mesh=mesh,
        in_specs=(tile, tile, tile) + (P(),) * 7,
        out_specs=(tile, tile, rows, rows),
        check_vma=False,
    )
```

```python
import functools

import jax
import jax.numpy as jnp
import numpy as np
from jax import lax
from jax.experimental import pallas as pl
from jax.experimental.pallas import tpu as pltpu
from jax.sharding import PartitionSpec as P

BF = jnp.bfloat16
F32 = jnp.float32


def dot(a, b):
    return jnp.dot(a, b, preferred_element_type=F32)


def dot_nt(a, b):
    return lax.dot_general(a, b, (((1,), (1,)), ((), ())), preferred_element_type=F32)


def dot_tn(a, b):
    return lax.dot_general(a, b, (((0,), (0,)), ((), ())), preferred_element_type=F32)


def call(body, outs, *args, mib=24, scratch=(), hbm=(), pin=True, cost=0, aliases=None):
    vmem = pl.BlockSpec(memory_space=pltpu.VMEM)
    far = pl.BlockSpec(memory_space=pltpu.HBM)
    in_specs = [far if i in hbm else vmem for i in range(len(args))]
    args = [pltpu.with_memory_space_constraint(a, pltpu.HBM) if i in hbm else a for i, a in enumerate(args)]
    return pl.pallas_call(
        body,
        out_shape=[pltpu.VMEM(s, d) if pin else jax.ShapeDtypeStruct(s, d) for s, d in outs],
        in_specs=in_specs,
        out_specs=[vmem] * len(outs),
        scratch_shapes=list(scratch),
        input_output_aliases=aliases or {},
        compiler_params=pltpu.CompilerParams(vmem_limit_bytes=mib * 2**20),
        cost_estimate=pl.CostEstimate(flops=cost * 10**9, bytes_accessed=0, transcendentals=0),
    )(*args)


def frame_matrices(side):
    cells = side * side
    out = np.zeros((3, (side + 2) * side, cells + 4 * side), np.float32)
    for b in range(3):
        for r in range(side + 2):
            for j in range(side):
                c = j + b
                inner_r, inner_c = 1 <= r <= side, 1 <= c <= side
                if inner_r and inner_c:
                    src = (r - 1) * side + c - 1
                elif inner_c:
                    src = cells + (0 if r == 0 else 2) * side + c - 1
                elif inner_r:
                    src = cells + (3 if c == 0 else 1) * side + r - 1
                else:
                    continue
                out[b, r * side + j, src] = 1
    return out


def tap_matrices(side):
    m, cells = frame_matrices(side), side * side
    taps = [m[b, a * side : a * side + cells].T for a in range(3) for b in range(3)]
    return np.stack(taps)


def choose(index, values):
    out = jnp.full(index.shape, values[0], jnp.int32)
    for k in range(1, 4):
        out = jnp.where(index == k, values[k], out)
    return out


def edge_cell(edge, i, side):
    last = side - 1
    return jnp.where(
        edge == 0, i, jnp.where(edge == 1, i * side + last, jnp.where(edge == 2, last * side + i, i * side))
    )


def route_kernel(side, tiles, p_in, f_in, s_in, x, h, xh, s_first, s_second, sel, place, turn, rim_sel, partner, flip, slot, sems):
    c = x.shape[1]
    loads = [(p_in, partner), (f_in, flip), (s_in, slot), (x, xh.at[:, :c]), (h, xh.at[:, c:])]
    loads = [pltpu.make_async_copy(a, b, sems.at[n]) for n, (a, b) in enumerate(loads)]
    for copy in loads:
        copy.start()
    for copy in loads[:3]:
        copy.wait()
    me = lax.axis_index("tile")
    holder = lax.fori_loop(0, tiles, lambda t, a: a + jnp.where(slot[t] == me, t, 0), jnp.int32(0))
    q, fl, up = [], [], []
    for e in range(4):
        p = partner[e, holder]
        q.append(p & 3)
        fl.append(flip[e, holder])
        up.append((slot[p >> 2] == (me ^ 1)).astype(jnp.int32))
    out_at, in_at = [], []
    for e in range(4):
        before = sum([jnp.where(up[o] == up[e], 1, 0) for o in range(e)], jnp.int32(0))
        lower = sum(
            [jnp.where((up[o] == up[e]) & (q[o] < q[e]), 1, 0) for o in range(4) if o != e], jnp.int32(0)
        )
        out_at.append(before + 2 * (1 - up[e]))
        in_at.append(lower + 2 * (1 - up[e]))
    send_edge = [sum(jnp.where(out_at[e] == k, e, 0) for e in range(4)) for k in range(4)]
    recv_edge = [sum(jnp.where(in_at[e] == k, e, 0) for e in range(4)) for k in range(4)]
    recv_flip = [sum(jnp.where(in_at[e] == k, fl[e], 0) for e in range(4)) for k in range(4)]
    cells, rim = side * side, 4 * side

    def parts(shape, dim):
        at = lax.broadcasted_iota(jnp.int32, shape, dim)
        return at // side, at % side

    def one_hot(shape, dim, where_to):
        hit = lax.broadcasted_iota(jnp.int32, shape, dim) == where_to
        return jnp.where(hit, 1.0, 0.0).astype(BF)

    k, i = parts((rim, cells), 0)
    chosen = one_hot((rim, cells), 1, edge_cell(choose(k, send_edge), i, side))
    sel[...] = chosen
    for copy in loads[3:]:
        copy.wait()
    picked = dot(chosen, xh[...]).astype(BF)
    s_first[...] = picked[: rim // 2]
    s_second[...] = picked[rim // 2 :]
    k, i = parts((cells, rim), 1)
    i = jnp.where(choose(k, recv_flip) == 1, side - 1 - i, i)
    place[...] = one_hot((cells, rim), 0, edge_cell(choose(k, recv_edge), i, side))
    k, i = parts((rim, rim), 1)
    i = jnp.where(choose(k, recv_flip) == 1, side - 1 - i, i)
    turn[...] = one_hot((rim, rim), 0, choose(k, recv_edge) * side + i)
    width = 2 * side + 2 * cells
    k, i = parts((rim, width), 0)
    e = choose(k, send_edge)
    at = jnp.where(
        e == 0,
        i,
        jnp.where(
            e == 2, side + i, jnp.where(e == 3, 2 * side + i * side, 2 * side + cells + i * side + side - 1)
        ),
    )
    rim_sel[...] = one_hot((rim, width), 1, at)


def frames(side, tile, strips, m0, m2, f):
    whole = jnp.concatenate([tile, strips], axis=0)
    f[0] = dot(m0[...], whole).astype(BF)
    f[1, :side] = strips[:side]
    f[1, side : side + side * side] = tile
    f[1, side + side * side :] = strips[2 * side : 3 * side]
    f[2] = dot(m2[...], whole).astype(BF)


def conv(side, f, w, lo, hi, col_lo=0, col_hi=None):
    cells = side * side
    cols = [f[b, a * side : a * side + cells, :] for a in range(3) for b in range(3)]
    rows = [w[t, lo:hi, col_lo:col_hi] for t in range(9)]
    return dot(jnp.concatenate(cols, axis=1), jnp.concatenate(rows, axis=0))


def start_loads(pairs, sems):
    copies = [pltpu.make_async_copy(a, b, sems.at[k]) for k, (a, b) in enumerate(pairs)]
    for copy in copies:
        copy.start()
    return copies


def gate_kernel(
    side, xh, rp, rn, turn, m0, m2, w, bias, sel, wc_in, bc_in, g_in, gate, rh, pack, s_next, s_prev, f, wc, bc, g, sems
):
    copies = start_loads([(wc_in, wc), (bc_in, bc), (g_in, g)], sems)
    c = xh.shape[1] // 2
    cells, rim = side * side, 4 * side
    strips = dot(turn[...], jnp.concatenate([rp[...], rn[...]], axis=0)).astype(BF)
    frames(side, xh[...], strips, m0, m2, f)
    act = jax.nn.sigmoid(conv(side, f, w, 0, 2 * c) + bias[...])
    gate[...] = act
    reset_h = (act[:, c:] * xh[:, c:].astype(F32)).astype(BF)
    rh[...] = reset_h
    pack[:cells] = xh[:, c:]
    pack[cells : cells + rim] = strips[:, :c]
    pack[cells + rim :] = strips[:, c:]
    picked = dot(sel[...], reset_h).astype(BF)
    s_next[...] = picked[: rim // 2]
    s_prev[...] = picked[rim // 2 :]
    for copy in copies:
        copy.wait()


def load_kernel(n, *refs):
    for copy in start_loads([(refs[k], refs[n + k]) for k in range(n)], refs[-1]):
        copy.wait()


def cand_x_kernel(side, f, w, bias, out):
    c = w.shape[2]
    cells = side * side
    cols = [f[b, a * side : a * side + cells, :c] for a in range(3) for b in range(3)]
    rows = [w[t, :c, :] for t in range(9)]
    out[...] = dot(jnp.concatenate(cols, axis=1), jnp.concatenate(rows, axis=0)) + bias[...]


def cand_kernel(side, acc, rh, rp, rn, turn, m0, m2, w, gate, h, g, d, d_u, f):
    c = g.shape[1]
    cells = side * side
    strips = dot(turn[...], jnp.concatenate([rp[...], rn[...]], axis=0)).astype(BF)
    frames(side, rh[...], strips, m0, m2, f)
    d_u[cells:] = strips
    candidate = jnp.tanh(acc[...] + conv(side, f, w, c, 2 * c))
    update = gate[:, :c]
    grad = g[...].astype(F32)
    d[...] = (grad * update * (1.0 - candidate * candidate)).astype(BF)
    d_u[:cells] = (grad * (candidate - h[:, c:].astype(F32)) * update * (1.0 - update)).astype(BF)


def spread(side, acc, d, w, lo, hi, col_lo, col_hi, fresh):
    cells = side * side
    if fresh:
        acc[...] = jnp.zeros_like(acc)
    for a in range(3):
        for b in range(3):
            rows = slice(a * side, a * side + cells)
            acc[b, rows, :] += dot_nt(d, w[a * 3 + b, lo:hi, col_lo:col_hi])


def gather_frame(side, acc):
    cells, c = side * side, acc.shape[2]
    rows = (side + 2) * side
    col = lax.broadcasted_iota(jnp.int32, (rows, c), 0) % side
    left, right = acc[0], acc[2]
    total = acc[1]
    total += jnp.where(col == side - 1, 0.0, pltpu.roll(left, rows - 1, 0))
    total += jnp.where(col == 0, 0.0, pltpu.roll(right, 1, 0))
    rim = jnp.concatenate(
        [total[:side], total[side + cells :], left[side : side + cells], right[side : side + cells]], axis=0
    ).astype(BF)
    return total[side : side + cells], rim


def back_rh_kernel(side, d, w, rim_sel, inner, s_next, s_prev, acc):
    c = w.shape[2]
    rim = 4 * side
    spread(side, acc, d[: side * side], w, c, 2 * c, 0, c, True)
    own, edge = gather_frame(side, acc)
    inner[...] = own
    picked = dot(rim_sel[...], edge).astype(BF)
    s_next[...] = picked[: rim // 2]
    s_prev[...] = picked[rim // 2 :]


def back_early_kernel(side, d, d_u, wc, wg, acc):
    c = wc.shape[2]
    cells = side * side
    acc[...] = jnp.zeros_like(acc)
    for a in range(3):
        for b in range(3):
            rows = slice(a * side, a * side + cells)
            t = a * 3 + b
            acc[b, rows, :c] += dot_nt(d[:cells], wc[t, :c, :]) + dot_nt(d_u[:cells], wg[t, :c, :c])
            acc[b, rows, c:] += dot_nt(d_u[:cells], wg[t, c:, :c])


def reset_kernel(side, inner, rp, rn, place, gate, h, g, d_c, d, direct):
    c = g.shape[1]
    d_rh = inner[...] + dot(place[...], jnp.concatenate([rp[...], rn[...]], axis=0))
    update, reset = gate[:, :c], gate[:, c:]
    cells = side * side
    d[:cells] = d_c[...]
    d[cells:] = (d_rh * h[:, c:].astype(F32) * reset * (1.0 - reset)).astype(BF)
    direct[...] = g[...].astype(F32) * (1.0 - update) + d_rh * reset


def back_gate_kernel(side, early, d, w, direct, rim_sel, inner, s_next, s_prev, acc):
    c = d.shape[1]
    rim = 4 * side
    acc[...] = early[...]
    cells = side * side
    spread(side, acc, d[cells:], w, 0, 2 * c, c, 2 * c, False)
    own, edge = gather_frame(side, acc)
    inner[:, :c] = own[:, :c]
    inner[:, c:] = own[:, c:] + direct[...]
    picked = dot(rim_sel[...], edge).astype(BF)
    s_next[...] = picked[: rim // 2]
    s_prev[...] = picked[rim // 2 :]


def final_kernel(inner, rp, rn, place, gx, gh):
    c = gx.shape[1]
    total = inner[...] + dot(place[...], jnp.concatenate([rp[...], rn[...]], axis=0))
    gx[...] = total[:, :c].astype(BF)
    gh[...] = total[:, c:].astype(BF)


def near_reset_kernel(side, *refs):
    x, packs, (m0, m2, w, bias, taps_in, out, taps, f, sems) = refs[1:4], refs[5:8], refs[8:]
    (copy,) = start_loads([(taps_in, taps)], sems)
    cells, rim, c = side * side, 4 * side, out.shape[2]
    for n in range(3):
        tile = jnp.concatenate([x[n][...], packs[n][:cells]], axis=1)
        strips = jnp.concatenate([packs[n][cells : cells + rim], packs[n][cells + rim :]], axis=1)
        frames(side, tile, strips, m0, m2, f.at[n])
    cols = [
        jnp.concatenate([f[n, b, a * side : a * side + cells, :] for n in range(3)], axis=0)
        for a in range(3)
        for b in range(3)
    ]
    rows = [w[t, :, c:] for t in range(9)]
    reset = jax.nn.sigmoid(dot(jnp.concatenate(cols, axis=1), jnp.concatenate(rows, axis=0)) + bias[:, c:])
    for n in range(3):
        out[n] = (reset[n * cells : (n + 1) * cells] * packs[n][:cells].astype(F32)).astype(BF)
    copy.wait()


def lhs_kernel(side, rows, tiles, cand, *refs):
    x, packs, more = refs[:4], refs[4:8], refs[8:-4]
    me = lax.axis_index("tile")
    taps, out, src, turned = refs[-4:]
    cells, rim = side * side, 4 * side
    c = packs[0].shape[1]
    per_tap = 2 * c // 128
    for n in range(4):
        lanes = slice(n * 128, (n + 1) * 128)
        for k in range(per_tap):
            at = slice(k * 128, (k + 1) * 128)
            col = slice(at.start % c, at.start % c + 128)
            if at.start < c:
                src[k, :cells, lanes] = x[n][:, col]
                src[k, cells:, lanes] = packs[n][cells : cells + rim, col]
            elif cand:
                rh, rh_near, ds = more[0], more[1], more[2:]
                src[k, :cells, lanes] = rh[:, col] if n == 0 else rh_near[n - 1, :, col]
                src[k, cells:, lanes] = ds[n][cells:, col]
            else:
                src[k, :cells, lanes] = packs[n][:cells, col]
                src[k, cells:, lanes] = packs[n][cells + rim :, col]
    for k in range(per_tap):
        turned[k] = src[k].T
    for t in range(out.shape[0]):
        target = me ^ (8 * (t // 2) + t % 2)
        for n in range(out.shape[1] // 128):
            block = jnp.minimum(target * rows // 128 + n, 9 * per_tap - 1)
            part = dot(turned[block % per_tap], taps[block // per_tap]).astype(BF)
            for k in range(4):
                out[t, n * 128 : (n + 1) * 128, k * cells : (k + 1) * cells] = part[k * 128 : (k + 1) * 128]


def weight_kernel(side, rows, parts, *refs):
    n = len(parts)
    lhs, ds, keep, sends, acc = refs[:n], refs[n : n + 4], refs[n + 4], refs[n + 5 : -1], refs[-1]
    cells = side * side
    c, width = ds[0].shape[1], sends[0].shape[2]
    me = lax.axis_index("tile")
    right = [jnp.concatenate([d[k * cells : (k + 1) * cells] for d in ds], axis=0) for k in parts]
    for t in range(lhs[0].shape[0]):
        target = me ^ (8 * (t // 2) + t % 2)
        first = pl.multiple_of(target * rows % 128, 8)
        for k in range(n):
            acc[k, t % 2] = dot(lhs[k][t], right[k])
            part = acc[k, t % 2, pl.ds(first, rows), :]
            if t % 2 == 0:
                keep[t // 2, :, k * c : (k + 1) * c] = part
            else:
                for j in range(c // width):
                    sends[k * (c // width) + j][t // 2] = part[:, j * width : (j + 1) * width].astype(BF)


def pair_kernel(*refs):
    own, far = refs[-2:]
    keep, first, at = None, 0, 0
    for r in refs[:-2]:
        if r.dtype == F32:
            keep, at = r, 0
            continue
        c = r.shape[2]
        cols = slice(first, first + c)
        own[:, cols] = keep[0, :, at : at + c] + r[0].astype(F32)
        for m in range(1, keep.shape[0]):
            far[m - 1, :, cols] = (keep[m, :, at : at + c] + r[m].astype(F32)).astype(BF)
        at, first = at + c, first + c


def sum_kernel(*refs):
    total = refs[0][...]
    for r in refs[1:-1]:
        total += r[...].astype(F32)
    refs[-1][...] = total


def sum_gate_kernel(update, *refs):
    parts, gate = refs[:-1], refs[-1]
    c = update.shape[1]
    total = parts[0][...]
    for r in parts[1:]:
        total += r[...].astype(F32)
    gate[:, :c] = update[...]
    gate[:, c:] = total


def shards(
    x_tiles, h_tiles, grad_out, w_gate, b_gate, w_cand, b_cand, partner_edge, edge_flip, tile_slot
):
    side, c = x_tiles.shape[1], x_tiles.shape[3]
    tiles = lax.axis_size("tile")
    cells, rim = side * side, 4 * side
    half, band = rim // 2, (side + 2) * side
    rows = 18 * c // tiles
    groups = tiles // 8
    blocks = max((rows * j + rows - 1) // 128 - rows * j // 128 + 1 for j in range(tiles)) * 128
    x, h, g = (u.reshape(cells, c) for u in (x_tiles, h_tiles, grad_out))
    wg, wc = w_gate.reshape(9, 2 * c, 2 * c), w_cand.reshape(9, 2 * c, c)
    bg, bc = b_gate.reshape(1, 2 * c), b_cand.reshape(1, c)
    m = frame_matrices(side)
    m0, m2 = jnp.asarray(m[0], BF), jnp.asarray(m[2], BF)
    taps = jnp.asarray(tap_matrices(side), BF)
    cross = [(i, (i + 1) % tiles if i % 2 else (i - 1) % tiles) for i in range(tiles)]
    ran = []

    def run(name, body, outs, *args, **options):
        if ran:
            args = (after(args[0], ran[-1]),) + args[1:]
        with jax.named_scope(name):
            results = call(body, outs, *args, **options)
        ran.append(results[0])
        return results

    def load(name, *args):
        n = len(args)
        return run(
            name, functools.partial(load_kernel, n), [(a.shape, a.dtype) for a in args], *args,
            hbm=range(n), scratch=[pltpu.SemaphoreType.DMA((n,))],
        )

    def after(u, *others):
        return lax.optimization_barrier((u,) + others)[0]

    def swap(u, k):
        return lax.ppermute(u, "tile", [(i, i ^ k) for i in range(tiles)])

    def exchange(s_first, s_second):
        return swap(s_first, 1), lax.ppermute(s_second, "tile", cross)

    def near(u):
        return [u] + [swap(u, k) for k in (2, 4, 6)]

    def lhs_of(name, cand, *args, cost=0):
        return run(
            name, functools.partial(lhs_kernel, side, rows, tiles, cand),
            [((2 * groups, blocks, 4 * cells), BF)],
            *args, taps_v,
            scratch=[
                pltpu.VMEM((2 * c // 128, cells + rim, 512), BF),
                pltpu.VMEM((2 * c // 128, 512, cells + rim), BF),
            ],
            cost=cost,
        )[0]

    def products(name, parts, lhs, ds, cuts=1, cost=0):
        n = len(parts)
        keep, *sends = run(
            name, functools.partial(weight_kernel, side, rows, parts),
            [((groups, rows, n * c), F32)] + [((groups, rows, c // cuts), BF)] * (n * cuts),
            *lhs, *ds,
            scratch=[pltpu.VMEM((n, 2, blocks, c), F32)],
            cost=cost,
        )
        return [keep] + [swap(u, 1) for u in sends]

    def pair(name, *sums, cost=0):
        n = sum(u.shape[2] for u in sums if u.dtype == F32)
        own, far = run(
            name, pair_kernel, [((rows, n), F32), ((groups - 1, rows, n), BF)], *sums, cost=cost
        )
        return [own] + [swap(far[k - 1], 8 * k) for k in range(1, groups)]

    xh, s1n, s1p, sel, place, turn, rim_sel = run(
        "route", functools.partial(route_kernel, side, tiles),
        [
            ((cells, 2 * c), BF),
            ((half, 2 * c), BF),
            ((half, 2 * c), BF),
            ((rim, cells), BF),
            ((cells, rim), BF),
            ((rim, rim), BF),
            ((rim, 2 * side + 2 * cells), BF),
        ],
        partner_edge.T, edge_flip.T, tile_slot, x, h,
        hbm=(0, 1, 2, 3, 4),
        scratch=[
            pltpu.SMEM((4, tiles), jnp.int32),
            pltpu.SMEM((4, tiles), jnp.int32),
            pltpu.SMEM((tiles,), jnp.int32),
            pltpu.SemaphoreType.DMA((5,)),
        ],
    )
    r1p, r1n = exchange(s1n, s1p)
    x_near = near(x)
    wg_v, m0, m2, bg_v = load("load_gate", wg, m0, m2, bg)
    gate, rh, pack, s2n, s2p, f, wc_v, bc_v, g_v = run(
        "gate", functools.partial(gate_kernel, side),
        [
            ((cells, 2 * c), F32),
            ((cells, c), BF),
            ((cells + 2 * rim, c), BF),
            ((half, c), BF),
            ((half, c), BF),
            ((3, band, 2 * c), BF),
            (wc.shape, BF),
            (bc.shape, F32),
            (g.shape, BF),
        ],
        after(xh, *x_near), r1p, r1n, turn, m0, m2, wg_v, bg_v, sel, wc, bc, g,
        hbm=(9, 10, 11), scratch=[pltpu.SemaphoreType.DMA((3,))], cost=5,
    )
    r2p, r2n = exchange(s2n, s2p)
    pack_near = near(after(pack, *x_near))
    (acc_x,) = run("cand_x", functools.partial(cand_x_kernel, side), [((cells, c), F32)], f, wc_v, bc_v)
    d_c, d_u, _ = run(
        "cand", functools.partial(cand_kernel, side),
        [((cells, c), BF), ((cells + rim, c), BF), ((3, band, c), BF)],
        acc_x, rh, r2p, r2n, turn, m0, m2, wc_v, gate, xh, g_v, cost=3,
    )
    inner_rh, s3n, s3p, _ = run(
        "back_rh", functools.partial(back_rh_kernel, side),
        [((cells, c), F32), ((half, c), BF), ((half, c), BF), ((3, band, c), F32)],
        d_c, wc_v, rim_sel,
    )
    r3p, r3n = exchange(s3n, s3p)
    u_near = near(after(d_u, s3n, *pack_near))
    rh_near, taps_v = run(
        "near_reset", functools.partial(near_reset_kernel, side), [((3, cells, c), BF), (taps.shape, BF)],
        *x_near, *pack_near, m0, m2, wg_v, bg_v, taps,
        hbm=(12,),
        scratch=[pltpu.VMEM((3, 3, band, 2 * c), BF), pltpu.SemaphoreType.DMA((1,))], cost=0,
    )
    d_cr, direct = run(
        "reset", functools.partial(reset_kernel, side),
        [((2 * cells, c), BF), ((cells, c), F32)],
        inner_rh, r3p, r3n, place, gate, xh, g_v, d_c, cost=5,
    )
    d_near = near(d_cr)
    lhs_gate = lhs_of("lhs_gate", False, *x_near, *pack_near, cost=0)
    sums_u = products("weights_update", (0,), [lhs_gate], u_near, cuts=2, cost=0)
    lhs_cand = lhs_of("lhs_cand", True, *x_near, *pack_near, rh, rh_near, *u_near, cost=0)
    parts_u = pair("pair_update", *sums_u)
    (early,) = run(
        "back_early", functools.partial(back_early_kernel, side), [((3, band, 2 * c), F32)], d_c, d_u, wc_v, wg_v
    )
    inner, s4n, s4p, _ = run(
        "back_gate", functools.partial(back_gate_kernel, side),
        [((cells, 2 * c), F32), ((half, 2 * c), BF), ((half, 2 * c), BF), ((3, band, 2 * c), F32)],
        early, d_cr, wg_v, direct, rim_sel,
    )
    r4p, r4n = exchange(s4n, s4p)
    sums_r = products("weights_reset", (1,), [lhs_gate], d_near, cuts=1, cost=0)
    sums_c = products("weights_cand", (0,), [lhs_cand], d_near, cuts=2, cost=0)
    (sum_u,) = run("sum_update", sum_kernel, [((rows, c), F32)], *parts_u, cost=2)
    parts_r = pair("pair_reset", *sums_r)
    parts_c = pair("pair_cand", *sums_c)
    (grad_w_gate,) = run(
        "sum_gate", sum_gate_kernel, [((rows, 2 * c), F32)], sum_u, *parts_r, pin=False, cost=0
    )
    gx, gh = run(
        "final", final_kernel, [((cells, c), BF), ((cells, c), BF)], inner, r4p, r4n, place, pin=False, cost=3
    )
    (grad_w_cand,) = run("sum_cand", sum_kernel, [((rows, c), F32)], *parts_c, pin=False)
    shape = (1, side, side, c)
    return gx.reshape(shape), gh.reshape(shape), grad_w_gate, grad_w_cand


def solution(mesh):
    tile = P(("grp", "tile"), None, None, None)
    rows = P(("grp", "tile"), None)
    return jax.shard_map(
        shards,
        mesh=mesh,
        in_specs=(tile, tile, tile) + (P(),) * 7,
        out_specs=(tile, tile, rows, rows),
        check_vma=False,
    )
```

```python
import functools

import jax
import jax.numpy as jnp
import numpy as np
from jax import lax
from jax.experimental import pallas as pl
from jax.experimental.pallas import tpu as pltpu
from jax.sharding import PartitionSpec as P

BF = jnp.bfloat16
F32 = jnp.float32


def dot(a, b):
    return jnp.dot(a, b, preferred_element_type=F32)


def dot_nt(a, b):
    return lax.dot_general(a, b, (((1,), (1,)), ((), ())), preferred_element_type=F32)


def dot_tn(a, b):
    return lax.dot_general(a, b, (((0,), (0,)), ((), ())), preferred_element_type=F32)


def call(body, outs, *args, mib=24, scratch=(), hbm=(), pin=True, cost=0, aliases=None):
    vmem = pl.BlockSpec(memory_space=pltpu.VMEM)
    far = pl.BlockSpec(memory_space=pltpu.HBM)
    in_specs = [far if i in hbm else vmem for i in range(len(args))]
    args = [pltpu.with_memory_space_constraint(a, pltpu.HBM) if i in hbm else a for i, a in enumerate(args)]
    return pl.pallas_call(
        body,
        out_shape=[pltpu.VMEM(s, d) if pin else jax.ShapeDtypeStruct(s, d) for s, d in outs],
        in_specs=in_specs,
        out_specs=[vmem] * len(outs),
        scratch_shapes=list(scratch),
        input_output_aliases=aliases or {},
        compiler_params=pltpu.CompilerParams(vmem_limit_bytes=mib * 2**20),
        cost_estimate=pl.CostEstimate(flops=cost * 10**9, bytes_accessed=0, transcendentals=0),
    )(*args)


def frame_matrices(side):
    cells = side * side
    out = np.zeros((3, (side + 2) * side, cells + 4 * side), np.float32)
    for b in range(3):
        for r in range(side + 2):
            for j in range(side):
                c = j + b
                inner_r, inner_c = 1 <= r <= side, 1 <= c <= side
                if inner_r and inner_c:
                    src = (r - 1) * side + c - 1
                elif inner_c:
                    src = cells + (0 if r == 0 else 2) * side + c - 1
                elif inner_r:
                    src = cells + (3 if c == 0 else 1) * side + r - 1
                else:
                    continue
                out[b, r * side + j, src] = 1
    return out


def tap_matrices(side):
    m, cells = frame_matrices(side), side * side
    taps = [m[b, a * side : a * side + cells].T for a in range(3) for b in range(3)]
    return np.stack(taps)


def choose(index, values):
    out = jnp.full(index.shape, values[0], jnp.int32)
    for k in range(1, 4):
        out = jnp.where(index == k, values[k], out)
    return out


def edge_cell(edge, i, side):
    last = side - 1
    return jnp.where(
        edge == 0, i, jnp.where(edge == 1, i * side + last, jnp.where(edge == 2, last * side + i, i * side))
    )


def route_kernel(side, tiles, p_in, f_in, s_in, x, h, xh, s_first, s_second, sel, place, turn, rim_sel, partner, flip, slot, sems):
    c = x.shape[1]
    loads = [(p_in, partner), (f_in, flip), (s_in, slot), (x, xh.at[:, :c]), (h, xh.at[:, c:])]
    loads = [pltpu.make_async_copy(a, b, sems.at[n]) for n, (a, b) in enumerate(loads)]
    for copy in loads:
        copy.start()
    for copy in loads[:3]:
        copy.wait()
    me = lax.axis_index("tile")
    holder = lax.fori_loop(0, tiles, lambda t, a: a + jnp.where(slot[t] == me, t, 0), jnp.int32(0))
    q, fl, up = [], [], []
    for e in range(4):
        p = partner[e, holder]
        q.append(p & 3)
        fl.append(flip[e, holder])
        up.append((slot[p >> 2] == (me ^ 1)).astype(jnp.int32))
    out_at, in_at = [], []
    for e in range(4):
        before = sum([jnp.where(up[o] == up[e], 1, 0) for o in range(e)], jnp.int32(0))
        lower = sum(
            [jnp.where((up[o] == up[e]) & (q[o] < q[e]), 1, 0) for o in range(4) if o != e], jnp.int32(0)
        )
        out_at.append(before + 2 * (1 - up[e]))
        in_at.append(lower + 2 * (1 - up[e]))
    send_edge = [sum(jnp.where(out_at[e] == k, e, 0) for e in range(4)) for k in range(4)]
    recv_edge = [sum(jnp.where(in_at[e] == k, e, 0) for e in range(4)) for k in range(4)]
    recv_flip = [sum(jnp.where(in_at[e] == k, fl[e], 0) for e in range(4)) for k in range(4)]
    cells, rim = side * side, 4 * side

    def parts(shape, dim):
        at = lax.broadcasted_iota(jnp.int32, shape, dim)
        return at // side, at % side

    def one_hot(shape, dim, where_to):
        hit = lax.broadcasted_iota(jnp.int32, shape, dim) == where_to
        return jnp.where(hit, 1.0, 0.0).astype(BF)

    k, i = parts((rim, cells), 0)
    chosen = one_hot((rim, cells), 1, edge_cell(choose(k, send_edge), i, side))
    sel[...] = chosen
    for copy in loads[3:]:
        copy.wait()
    picked = dot(chosen, xh[...]).astype(BF)
    s_first[...] = picked[: rim // 2]
    s_second[...] = picked[rim // 2 :]
    k, i = parts((cells, rim), 1)
    i = jnp.where(choose(k, recv_flip) == 1, side - 1 - i, i)
    place[...] = one_hot((cells, rim), 0, edge_cell(choose(k, recv_edge), i, side))
    k, i = parts((rim, rim), 1)
    i = jnp.where(choose(k, recv_flip) == 1, side - 1 - i, i)
    turn[...] = one_hot((rim, rim), 0, choose(k, recv_edge) * side + i)
    width = 2 * side + 2 * cells
    k, i = parts((rim, width), 0)
    e = choose(k, send_edge)
    at = jnp.where(
        e == 0,
        i,
        jnp.where(
            e == 2, side + i, jnp.where(e == 3, 2 * side + i * side, 2 * side + cells + i * side + side - 1)
        ),
    )
    rim_sel[...] = one_hot((rim, width), 1, at)


def frames(side, tile, strips, m0, m2, f):
    whole = jnp.concatenate([tile, strips], axis=0)
    f[0] = dot(m0[...], whole).astype(BF)
    f[1, :side] = strips[:side]
    f[1, side : side + side * side] = tile
    f[1, side + side * side :] = strips[2 * side : 3 * side]
    f[2] = dot(m2[...], whole).astype(BF)


def conv(side, f, w, lo, hi, col_lo=0, col_hi=None):
    cells = side * side
    cols = [f[b, a * side : a * side + cells, :] for a in range(3) for b in range(3)]
    rows = [w[t, lo:hi, col_lo:col_hi] for t in range(9)]
    return dot(jnp.concatenate(cols, axis=1), jnp.concatenate(rows, axis=0))


def start_loads(pairs, sems):
    copies = [pltpu.make_async_copy(a, b, sems.at[k]) for k, (a, b) in enumerate(pairs)]
    for copy in copies:
        copy.start()
    return copies


def gate_kernel(
    side, xh, rp, rn, turn, m0, m2, w, bias, sel, wc_in, bc_in, g_in, gate, rh, pack, s_next, s_prev, f, wc, bc, g, sems
):
    copies = start_loads([(wc_in, wc), (bc_in, bc), (g_in, g)], sems)
    c = xh.shape[1] // 2
    cells, rim = side * side, 4 * side
    strips = dot(turn[...], jnp.concatenate([rp[...], rn[...]], axis=0)).astype(BF)
    frames(side, xh[...], strips, m0, m2, f)
    act = jax.nn.sigmoid(conv(side, f, w, 0, 2 * c) + bias[...])
    gate[...] = act
    reset_h = (act[:, c:] * xh[:, c:].astype(F32)).astype(BF)
    rh[...] = reset_h
    pack[:cells] = xh[:, c:]
    pack[cells : cells + rim] = strips[:, :c]
    pack[cells + rim :] = strips[:, c:]
    picked = dot(sel[...], reset_h).astype(BF)
    s_next[...] = picked[: rim // 2]
    s_prev[...] = picked[rim // 2 :]
    for copy in copies:
        copy.wait()


def load_kernel(n, *refs):
    for copy in start_loads([(refs[k], refs[n + k]) for k in range(n)], refs[-1]):
        copy.wait()


def cand_x_kernel(side, f, w, bias, out):
    c = w.shape[2]
    cells = side * side
    cols = [f[b, a * side : a * side + cells, :c] for a in range(3) for b in range(3)]
    rows = [w[t, :c, :] for t in range(9)]
    out[...] = dot(jnp.concatenate(cols, axis=1), jnp.concatenate(rows, axis=0)) + bias[...]


def cand_kernel(side, acc, rh, rp, rn, turn, m0, m2, w, gate, h, g, d, d_u, f):
    c = g.shape[1]
    cells = side * side
    strips = dot(turn[...], jnp.concatenate([rp[...], rn[...]], axis=0)).astype(BF)
    frames(side, rh[...], strips, m0, m2, f)
    d_u[cells:] = strips
    candidate = jnp.tanh(acc[...] + conv(side, f, w, c, 2 * c))
    update = gate[:, :c]
    grad = g[...].astype(F32)
    d[...] = (grad * update * (1.0 - candidate * candidate)).astype(BF)
    d_u[:cells] = (grad * (candidate - h[:, c:].astype(F32)) * update * (1.0 - update)).astype(BF)


def spread(side, acc, d, w, lo, hi, col_lo, col_hi, fresh):
    cells = side * side
    if fresh:
        acc[...] = jnp.zeros_like(acc)
    for a in range(3):
        for b in range(3):
            rows = slice(a * side, a * side + cells)
            acc[b, rows, :] += dot_nt(d, w[a * 3 + b, lo:hi, col_lo:col_hi])


def gather_frame(side, acc):
    cells, c = side * side, acc.shape[2]
    rows = (side + 2) * side
    col = lax.broadcasted_iota(jnp.int32, (rows, c), 0) % side
    left, right = acc[0], acc[2]
    total = acc[1]
    total += jnp.where(col == side - 1, 0.0, pltpu.roll(left, rows - 1, 0))
    total += jnp.where(col == 0, 0.0, pltpu.roll(right, 1, 0))
    rim = jnp.concatenate(
        [total[:side], total[side + cells :], left[side : side + cells], right[side : side + cells]], axis=0
    ).astype(BF)
    return total[side : side + cells], rim


def back_rh_kernel(side, d, w, rim_sel, inner, s_next, s_prev, acc):
    c = w.shape[2]
    rim = 4 * side
    spread(side, acc, d[: side * side], w, c, 2 * c, 0, c, True)
    own, edge = gather_frame(side, acc)
    inner[...] = own
    picked = dot(rim_sel[...], edge).astype(BF)
    s_next[...] = picked[: rim // 2]
    s_prev[...] = picked[rim // 2 :]


def back_early_kernel(side, d, d_u, wc, wg, acc):
    c = wc.shape[2]
    cells = side * side
    acc[...] = jnp.zeros_like(acc)
    for a in range(3):
        for b in range(3):
            rows = slice(a * side, a * side + cells)
            t = a * 3 + b
            acc[b, rows, :c] += dot_nt(d[:cells], wc[t, :c, :]) + dot_nt(d_u[:cells], wg[t, :c, :c])
            acc[b, rows, c:] += dot_nt(d_u[:cells], wg[t, c:, :c])


def reset_kernel(side, inner, rp, rn, place, gate, h, g, d_c, d, direct):
    c = g.shape[1]
    d_rh = inner[...] + dot(place[...], jnp.concatenate([rp[...], rn[...]], axis=0))
    update, reset = gate[:, :c], gate[:, c:]
    cells = side * side
    d[:cells] = d_c[...]
    d[cells:] = (d_rh * h[:, c:].astype(F32) * reset * (1.0 - reset)).astype(BF)
    direct[...] = g[...].astype(F32) * (1.0 - update) + d_rh * reset


def back_gate_kernel(side, early, d, w, direct, rim_sel, inner, s_next, s_prev, acc):
    c = d.shape[1]
    rim = 4 * side
    acc[...] = early[...]
    cells = side * side
    spread(side, acc, d[cells:], w, 0, 2 * c, c, 2 * c, False)
    own, edge = gather_frame(side, acc)
    inner[:, :c] = own[:, :c]
    inner[:, c:] = own[:, c:] + direct[...]
    picked = dot(rim_sel[...], edge).astype(BF)
    s_next[...] = picked[: rim // 2]
    s_prev[...] = picked[rim // 2 :]


def final_kernel(inner, rp, rn, place, gx, gh):
    c = gx.shape[1]
    total = inner[...] + dot(place[...], jnp.concatenate([rp[...], rn[...]], axis=0))
    gx[...] = total[:, :c].astype(BF)
    gh[...] = total[:, c:].astype(BF)


def near_reset_kernel(side, *refs):
    x, packs, (m0, m2, w, bias, taps_in, out, taps, f, sems) = refs[1:4], refs[5:8], refs[8:]
    (copy,) = start_loads([(taps_in, taps)], sems)
    cells, rim, c = side * side, 4 * side, out.shape[2]
    for n in range(3):
        tile = jnp.concatenate([x[n][...], packs[n][:cells]], axis=1)
        strips = jnp.concatenate([packs[n][cells : cells + rim], packs[n][cells + rim :]], axis=1)
        frames(side, tile, strips, m0, m2, f.at[n])
    cols = [
        jnp.concatenate([f[n, b, a * side : a * side + cells, :] for n in range(3)], axis=0)
        for a in range(3)
        for b in range(3)
    ]
    rows = [w[t, :, c:] for t in range(9)]
    reset = jax.nn.sigmoid(dot(jnp.concatenate(cols, axis=1), jnp.concatenate(rows, axis=0)) + bias[:, c:])
    for n in range(3):
        out[n] = (reset[n * cells : (n + 1) * cells] * packs[n][:cells].astype(F32)).astype(BF)
    copy.wait()


def lhs_kernel(side, rows, tiles, cand, *refs):
    x, packs, more = refs[:4], refs[4:8], refs[8:-4]
    me = lax.axis_index("tile")
    taps, out, src, turned = refs[-4:]
    cells, rim = side * side, 4 * side
    c = packs[0].shape[1]
    per_tap = 2 * c // 128
    for n in range(4):
        lanes = slice(n * 128, (n + 1) * 128)
        for k in range(per_tap):
            at = slice(k * 128, (k + 1) * 128)
            col = slice(at.start % c, at.start % c + 128)
            if at.start < c:
                src[k, :cells, lanes] = x[n][:, col]
                src[k, cells:, lanes] = packs[n][cells : cells + rim, col]
            elif cand:
                rh, rh_near, ds = more[0], more[1], more[2:]
                src[k, :cells, lanes] = rh[:, col] if n == 0 else rh_near[n - 1, :, col]
                src[k, cells:, lanes] = ds[n][cells:, col]
            else:
                src[k, :cells, lanes] = packs[n][:cells, col]
                src[k, cells:, lanes] = packs[n][cells + rim :, col]
    for k in range(per_tap):
        turned[k] = src[k].T
    for t in range(out.shape[0]):
        target = me ^ (8 * (t // 2) + t % 2)
        for n in range(out.shape[1] // 128):
            block = jnp.minimum(target * rows // 128 + n, 9 * per_tap - 1)
            part = dot(turned[block % per_tap], taps[block // per_tap]).astype(BF)
            for k in range(4):
                out[t, n * 128 : (n + 1) * 128, k * cells : (k + 1) * cells] = part[k * 128 : (k + 1) * 128]


def weight_kernel(side, rows, parts, *refs):
    n = len(parts)
    lhs, ds, keep, sends, acc = refs[:n], refs[n : n + 4], refs[n + 4], refs[n + 5 : -1], refs[-1]
    cells = side * side
    c, width = ds[0].shape[1], sends[0].shape[2]
    me = lax.axis_index("tile")
    right = [jnp.concatenate([d[k * cells : (k + 1) * cells] for d in ds], axis=0) for k in parts]
    for t in range(lhs[0].shape[0]):
        target = me ^ (8 * (t // 2) + t % 2)
        first = pl.multiple_of(target * rows % 128, 8)
        for k in range(n):
            acc[k, t % 2] = dot(lhs[k][t], right[k])
            part = acc[k, t % 2, pl.ds(first, rows), :]
            if t % 2 == 0:
                keep[t // 2, :, k * c : (k + 1) * c] = part
            else:
                for j in range(c // width):
                    sends[k * (c // width) + j][t // 2] = part[:, j * width : (j + 1) * width].astype(BF)


def pair_kernel(*refs):
    own, far = refs[-2:]
    keep, first, at = None, 0, 0
    for r in refs[:-2]:
        if r.dtype == F32:
            keep, at = r, 0
            continue
        c = r.shape[2]
        cols = slice(first, first + c)
        own[:, cols] = keep[0, :, at : at + c] + r[0].astype(F32)
        for m in range(1, keep.shape[0]):
            far[m - 1, :, cols] = (keep[m, :, at : at + c] + r[m].astype(F32)).astype(BF)
        at, first = at + c, first + c


def sum_kernel(*refs):
    total = refs[0][...]
    for r in refs[1:-1]:
        total += r[...].astype(F32)
    refs[-1][...] = total


def sum_gate_kernel(update, *refs):
    parts, gate = refs[:-1], refs[-1]
    c = update.shape[1]
    total = parts[0][...]
    for r in parts[1:]:
        total += r[...].astype(F32)
    gate[:, :c] = update[...]
    gate[:, c:] = total


def shards(
    x_tiles, h_tiles, grad_out, w_gate, b_gate, w_cand, b_cand, partner_edge, edge_flip, tile_slot
):
    side, c = x_tiles.shape[1], x_tiles.shape[3]
    tiles = lax.axis_size("tile")
    cells, rim = side * side, 4 * side
    half, band = rim // 2, (side + 2) * side
    rows = 18 * c // tiles
    groups = tiles // 8
    blocks = max((rows * j + rows - 1) // 128 - rows * j // 128 + 1 for j in range(tiles)) * 128
    x, h, g = (u.reshape(cells, c) for u in (x_tiles, h_tiles, grad_out))
    wg, wc = w_gate.reshape(9, 2 * c, 2 * c), w_cand.reshape(9, 2 * c, c)
    bg, bc = b_gate.reshape(1, 2 * c), b_cand.reshape(1, c)
    m = frame_matrices(side)
    m0, m2 = jnp.asarray(m[0], BF), jnp.asarray(m[2], BF)
    taps = jnp.asarray(tap_matrices(side), BF)
    cross = [(i, (i + 1) % tiles if i % 2 else (i - 1) % tiles) for i in range(tiles)]
    ran = []

    def run(name, body, outs, *args, **options):
        if ran:
            args = (after(args[0], ran[-1]),) + args[1:]
        with jax.named_scope(name):
            results = call(body, outs, *args, **options)
        ran.append(results[0])
        return results

    def load(name, *args):
        n = len(args)
        return run(
            name, functools.partial(load_kernel, n), [(a.shape, a.dtype) for a in args], *args,
            hbm=range(n), scratch=[pltpu.SemaphoreType.DMA((n,))],
        )

    def after(u, *others):
        return lax.optimization_barrier((u,) + others)[0]

    def swap(u, k):
        return lax.ppermute(u, "tile", [(i, i ^ k) for i in range(tiles)])

    def exchange(s_first, s_second):
        return swap(s_first, 1), lax.ppermute(s_second, "tile", cross)

    def near(u):
        return [u] + [swap(u, k) for k in (2, 4, 6)]

    def lhs_of(name, cand, *args, cost=0):
        return run(
            name, functools.partial(lhs_kernel, side, rows, tiles, cand),
            [((2 * groups, blocks, 4 * cells), BF)],
            *args, taps_v,
            scratch=[
                pltpu.VMEM((2 * c // 128, cells + rim, 512), BF),
                pltpu.VMEM((2 * c // 128, 512, cells + rim), BF),
            ],
            cost=cost,
        )[0]

    def products(name, parts, lhs, ds, cuts=1, cost=0):
        n = len(parts)
        keep, *sends = run(
            name, functools.partial(weight_kernel, side, rows, parts),
            [((groups, rows, n * c), F32)] + [((groups, rows, c // cuts), BF)] * (n * cuts),
            *lhs, *ds,
            scratch=[pltpu.VMEM((n, 2, blocks, c), F32)],
            cost=cost,
        )
        return [keep] + [swap(u, 1) for u in sends]

    def pair(name, *sums, cost=0):
        n = sum(u.shape[2] for u in sums if u.dtype == F32)
        own, far = run(
            name, pair_kernel, [((rows, n), F32), ((groups - 1, rows, n), BF)], *sums, cost=cost
        )
        return [own] + [swap(far[k - 1], 8 * k) for k in range(1, groups)]

    xh, s1n, s1p, sel, place, turn, rim_sel = run(
        "route", functools.partial(route_kernel, side, tiles),
        [
            ((cells, 2 * c), BF),
            ((half, 2 * c), BF),
            ((half, 2 * c), BF),
            ((rim, cells), BF),
            ((cells, rim), BF),
            ((rim, rim), BF),
            ((rim, 2 * side + 2 * cells), BF),
        ],
        partner_edge.T, edge_flip.T, tile_slot, x, h,
        hbm=(0, 1, 2, 3, 4),
        scratch=[
            pltpu.SMEM((4, tiles), jnp.int32),
            pltpu.SMEM((4, tiles), jnp.int32),
            pltpu.SMEM((tiles,), jnp.int32),
            pltpu.SemaphoreType.DMA((5,)),
        ],
    )
    r1p, r1n = exchange(s1n, s1p)
    x_near = near(x)
    wg_v, m0, m2, bg_v = load("load_gate", wg, m0, m2, bg)
    gate, rh, pack, s2n, s2p, f, wc_v, bc_v, g_v = run(
        "gate", functools.partial(gate_kernel, side),
        [
            ((cells, 2 * c), F32),
            ((cells, c), BF),
            ((cells + 2 * rim, c), BF),
            ((half, c), BF),
            ((half, c), BF),
            ((3, band, 2 * c), BF),
            (wc.shape, BF),
            (bc.shape, F32),
            (g.shape, BF),
        ],
        xh, r1p, r1n, turn, m0, m2, wg_v, bg_v, sel, wc, bc, g,
        hbm=(9, 10, 11), scratch=[pltpu.SemaphoreType.DMA((3,))], cost=5,
    )
    r2p, r2n = exchange(s2n, s2p)
    pack_near = near(after(pack, *x_near))
    (acc_x,) = run("cand_x", functools.partial(cand_x_kernel, side), [((cells, c), F32)], after(f, *x_near), wc_v, bc_v)
    d_c, d_u, _ = run(
        "cand", functools.partial(cand_kernel, side),
        [((cells, c), BF), ((cells + rim, c), BF), ((3, band, c), BF)],
        acc_x, rh, r2p, r2n, turn, m0, m2, wc_v, gate, xh, g_v, cost=3,
    )
    inner_rh, s3n, s3p, _ = run(
        "back_rh", functools.partial(back_rh_kernel, side),
        [((cells, c), F32), ((half, c), BF), ((half, c), BF), ((3, band, c), F32)],
        d_c, wc_v, rim_sel,
    )
    r3p, r3n = exchange(s3n, s3p)
    u_near = near(d_u)
    rh_near, taps_v = run(
        "near_reset", functools.partial(near_reset_kernel, side), [((3, cells, c), BF), (taps.shape, BF)],
        *x_near, *pack_near, m0, m2, wg_v, bg_v, taps,
        hbm=(12,),
        scratch=[pltpu.VMEM((3, 3, band, 2 * c), BF), pltpu.SemaphoreType.DMA((1,))], cost=0,
    )
    d_cr, direct = run(
        "reset", functools.partial(reset_kernel, side),
        [((2 * cells, c), BF), ((cells, c), F32)],
        inner_rh, r3p, r3n, place, gate, xh, g_v, d_c, cost=5,
    )
    d_near = near(d_cr)
    lhs_gate = lhs_of("lhs_gate", False, *x_near, *pack_near, cost=0)
    sums_u = products("weights_update", (0,), [lhs_gate], u_near, cuts=2, cost=0)
    lhs_cand = lhs_of("lhs_cand", True, *x_near, *pack_near, rh, rh_near, *u_near, cost=0)
    parts_u = pair("pair_update", *sums_u)
    (early,) = run(
        "back_early", functools.partial(back_early_kernel, side), [((3, band, 2 * c), F32)], d_c, d_u, wc_v, wg_v
    )
    inner, s4n, s4p, _ = run(
        "back_gate", functools.partial(back_gate_kernel, side),
        [((cells, 2 * c), F32), ((half, 2 * c), BF), ((half, 2 * c), BF), ((3, band, 2 * c), F32)],
        early, d_cr, wg_v, direct, rim_sel,
    )
    r4p, r4n = exchange(s4n, s4p)
    sums_r = products("weights_reset", (1,), [lhs_gate], d_near, cuts=1, cost=0)
    sums_c = products("weights_cand", (0,), [lhs_cand], d_near, cuts=2, cost=0)
    (sum_u,) = run("sum_update", sum_kernel, [((rows, c), F32)], *parts_u, cost=2)
    parts_r = pair("pair_reset", *sums_r)
    parts_c = pair("pair_cand", *sums_c)
    (grad_w_gate,) = run(
        "sum_gate", sum_gate_kernel, [((rows, 2 * c), F32)], sum_u, *parts_r, pin=False, cost=0
    )
    gx, gh = run(
        "final", final_kernel, [((cells, c), BF), ((cells, c), BF)], inner, r4p, r4n, place, pin=False, cost=3
    )
    (grad_w_cand,) = run("sum_cand", sum_kernel, [((rows, c), F32)], *parts_c, pin=False)
    shape = (1, side, side, c)
    return gx.reshape(shape), gh.reshape(shape), grad_w_gate, grad_w_cand


def solution(mesh):
    tile = P(("grp", "tile"), None, None, None)
    rows = P(("grp", "tile"), None)
    return jax.shard_map(
        shards,
        mesh=mesh,
        in_specs=(tile, tile, tile) + (P(),) * 7,
        out_specs=(tile, tile, rows, rows),
        check_vma=False,
    )
```

```python
import functools

import jax
import jax.numpy as jnp
import numpy as np
from jax import lax
from jax.experimental import pallas as pl
from jax.experimental.pallas import tpu as pltpu
from jax.sharding import PartitionSpec as P

BF = jnp.bfloat16
F32 = jnp.float32


def dot(a, b):
    return jnp.dot(a, b, preferred_element_type=F32)


def dot_nt(a, b):
    return lax.dot_general(a, b, (((1,), (1,)), ((), ())), preferred_element_type=F32)


def dot_tn(a, b):
    return lax.dot_general(a, b, (((0,), (0,)), ((), ())), preferred_element_type=F32)


def call(body, outs, *args, mib=24, scratch=(), hbm=(), pin=True, cost=0, aliases=None):
    vmem = pl.BlockSpec(memory_space=pltpu.VMEM)
    far = pl.BlockSpec(memory_space=pltpu.HBM)
    in_specs = [far if i in hbm else vmem for i in range(len(args))]
    args = [pltpu.with_memory_space_constraint(a, pltpu.HBM) if i in hbm else a for i, a in enumerate(args)]
    return pl.pallas_call(
        body,
        out_shape=[pltpu.VMEM(s, d) if pin else jax.ShapeDtypeStruct(s, d) for s, d in outs],
        in_specs=in_specs,
        out_specs=[vmem] * len(outs),
        scratch_shapes=list(scratch),
        input_output_aliases=aliases or {},
        compiler_params=pltpu.CompilerParams(vmem_limit_bytes=mib * 2**20),
        cost_estimate=pl.CostEstimate(flops=cost * 10**9, bytes_accessed=0, transcendentals=0),
    )(*args)


def frame_matrices(side):
    cells = side * side
    out = np.zeros((3, (side + 2) * side, cells + 4 * side), np.float32)
    for b in range(3):
        for r in range(side + 2):
            for j in range(side):
                c = j + b
                inner_r, inner_c = 1 <= r <= side, 1 <= c <= side
                if inner_r and inner_c:
                    src = (r - 1) * side + c - 1
                elif inner_c:
                    src = cells + (0 if r == 0 else 2) * side + c - 1
                elif inner_r:
                    src = cells + (3 if c == 0 else 1) * side + r - 1
                else:
                    continue
                out[b, r * side + j, src] = 1
    return out


def tap_matrices(side):
    m, cells = frame_matrices(side), side * side
    taps = [m[b, a * side : a * side + cells].T for a in range(3) for b in range(3)]
    return np.stack(taps)


def choose(index, values):
    out = jnp.full(index.shape, values[0], jnp.int32)
    for k in range(1, 4):
        out = jnp.where(index == k, values[k], out)
    return out


def edge_cell(edge, i, side):
    last = side - 1
    return jnp.where(
        edge == 0, i, jnp.where(edge == 1, i * side + last, jnp.where(edge == 2, last * side + i, i * side))
    )


def route_kernel(side, tiles, p_in, f_in, s_in, x, h, xh, front, s_first, s_second, sel, place, turn, rim_sel, partner, flip, slot, sems):
    c = x.shape[1]
    loads = [(p_in, partner), (f_in, flip), (s_in, slot), (x, xh.at[:, :c]), (h, xh.at[:, c:])]
    loads += [(x, front.at[:, :c]), (h.at[:, : c - 128], front.at[:, c:])]
    loads = [pltpu.make_async_copy(a, b, sems.at[n]) for n, (a, b) in enumerate(loads)]
    for copy in loads:
        copy.start()
    for copy in loads[:3]:
        copy.wait()
    me = lax.axis_index("tile")
    holder = lax.fori_loop(0, tiles, lambda t, a: a + jnp.where(slot[t] == me, t, 0), jnp.int32(0))
    q, fl, up = [], [], []
    for e in range(4):
        p = partner[e, holder]
        q.append(p & 3)
        fl.append(flip[e, holder])
        up.append((slot[p >> 2] == (me ^ 1)).astype(jnp.int32))
    out_at, in_at = [], []
    for e in range(4):
        before = sum([jnp.where(up[o] == up[e], 1, 0) for o in range(e)], jnp.int32(0))
        lower = sum(
            [jnp.where((up[o] == up[e]) & (q[o] < q[e]), 1, 0) for o in range(4) if o != e], jnp.int32(0)
        )
        out_at.append(before + 2 * (1 - up[e]))
        in_at.append(lower + 2 * (1 - up[e]))
    send_edge = [sum(jnp.where(out_at[e] == k, e, 0) for e in range(4)) for k in range(4)]
    recv_edge = [sum(jnp.where(in_at[e] == k, e, 0) for e in range(4)) for k in range(4)]
    recv_flip = [sum(jnp.where(in_at[e] == k, fl[e], 0) for e in range(4)) for k in range(4)]
    cells, rim = side * side, 4 * side

    def parts(shape, dim):
        at = lax.broadcasted_iota(jnp.int32, shape, dim)
        return at // side, at % side

    def one_hot(shape, dim, where_to):
        hit = lax.broadcasted_iota(jnp.int32, shape, dim) == where_to
        return jnp.where(hit, 1.0, 0.0).astype(BF)

    k, i = parts((rim, cells), 0)
    chosen = one_hot((rim, cells), 1, edge_cell(choose(k, send_edge), i, side))
    sel[...] = chosen
    for copy in loads[3:]:
        copy.wait()
    picked = dot(chosen, xh[...]).astype(BF)
    s_first[...] = picked[: rim // 2]
    s_second[...] = picked[rim // 2 :]
    k, i = parts((cells, rim), 1)
    i = jnp.where(choose(k, recv_flip) == 1, side - 1 - i, i)
    place[...] = one_hot((cells, rim), 0, edge_cell(choose(k, recv_edge), i, side))
    k, i = parts((rim, rim), 1)
    i = jnp.where(choose(k, recv_flip) == 1, side - 1 - i, i)
    turn[...] = one_hot((rim, rim), 0, choose(k, recv_edge) * side + i)
    width = 2 * side + 2 * cells
    k, i = parts((rim, width), 0)
    e = choose(k, send_edge)
    at = jnp.where(
        e == 0,
        i,
        jnp.where(
            e == 2, side + i, jnp.where(e == 3, 2 * side + i * side, 2 * side + cells + i * side + side - 1)
        ),
    )
    rim_sel[...] = one_hot((rim, width), 1, at)


def frames(side, tile, strips, m0, m2, f):
    whole = jnp.concatenate([tile, strips], axis=0)
    f[0] = dot(m0[...], whole).astype(BF)
    f[1, :side] = strips[:side]
    f[1, side : side + side * side] = tile
    f[1, side + side * side :] = strips[2 * side : 3 * side]
    f[2] = dot(m2[...], whole).astype(BF)


def conv(side, f, w, lo, hi, col_lo=0, col_hi=None):
    cells = side * side
    cols = [f[b, a * side : a * side + cells, :] for a in range(3) for b in range(3)]
    rows = [w[t, lo:hi, col_lo:col_hi] for t in range(9)]
    return dot(jnp.concatenate(cols, axis=1), jnp.concatenate(rows, axis=0))


def start_loads(pairs, sems):
    copies = [pltpu.make_async_copy(a, b, sems.at[k]) for k, (a, b) in enumerate(pairs)]
    for copy in copies:
        copy.start()
    return copies


def gate_kernel(
    side, xh, rp, rn, turn, m0, m2, w, bias, sel, wc_in, bc_in, g_in, gate, rh, pack, s_next, s_prev, f, wc, bc, g, sems
):
    copies = start_loads([(wc_in, wc), (bc_in, bc), (g_in, g)], sems)
    c = xh.shape[1] // 2
    cells, rim = side * side, 4 * side
    strips = dot(turn[...], jnp.concatenate([rp[...], rn[...]], axis=0)).astype(BF)
    frames(side, xh[...], strips, m0, m2, f)
    act = jax.nn.sigmoid(conv(side, f, w, 0, 2 * c) + bias[...])
    gate[...] = act
    reset_h = (act[:, c:] * xh[:, c:].astype(F32)).astype(BF)
    rh[...] = reset_h
    pack[:cells] = xh[:, 2 * c - 128 :]
    for k in range(2 * c // 128):
        pack[cells + k * rim : cells + (k + 1) * rim] = strips[:, k * 128 : (k + 1) * 128]
    picked = dot(sel[...], reset_h).astype(BF)
    s_next[...] = picked[: rim // 2]
    s_prev[...] = picked[rim // 2 :]
    for copy in copies:
        copy.wait()


def load_kernel(n, *refs):
    for copy in start_loads([(refs[k], refs[n + k]) for k in range(n)], refs[-1]):
        copy.wait()


def cand_x_kernel(side, f, w, bias, out):
    c = w.shape[2]
    cells = side * side
    cols = [f[b, a * side : a * side + cells, :c] for a in range(3) for b in range(3)]
    rows = [w[t, :c, :] for t in range(9)]
    out[...] = dot(jnp.concatenate(cols, axis=1), jnp.concatenate(rows, axis=0)) + bias[...]


def cand_kernel(side, acc, rh, rp, rn, turn, m0, m2, w, gate, h, g, d, d_u, f):
    c = g.shape[1]
    cells = side * side
    strips = dot(turn[...], jnp.concatenate([rp[...], rn[...]], axis=0)).astype(BF)
    frames(side, rh[...], strips, m0, m2, f)
    d_u[cells:] = strips
    candidate = jnp.tanh(acc[...] + conv(side, f, w, c, 2 * c))
    update = gate[:, :c]
    grad = g[...].astype(F32)
    d[...] = (grad * update * (1.0 - candidate * candidate)).astype(BF)
    d_u[:cells] = (grad * (candidate - h[:, c:].astype(F32)) * update * (1.0 - update)).astype(BF)


def spread(side, acc, d, w, lo, hi, col_lo, col_hi, fresh):
    cells = side * side
    if fresh:
        acc[...] = jnp.zeros_like(acc)
    for a in range(3):
        for b in range(3):
            rows = slice(a * side, a * side + cells)
            acc[b, rows, :] += dot_nt(d, w[a * 3 + b, lo:hi, col_lo:col_hi])


def gather_frame(side, acc):
    cells, c = side * side, acc.shape[2]
    rows = (side + 2) * side
    col = lax.broadcasted_iota(jnp.int32, (rows, c), 0) % side
    left, right = acc[0], acc[2]
    total = acc[1]
    total += jnp.where(col == side - 1, 0.0, pltpu.roll(left, rows - 1, 0))
    total += jnp.where(col == 0, 0.0, pltpu.roll(right, 1, 0))
    rim = jnp.concatenate(
        [total[:side], total[side + cells :], left[side : side + cells], right[side : side + cells]], axis=0
    ).astype(BF)
    return total[side : side + cells], rim


def back_rh_kernel(side, d, w, rim_sel, inner, s_next, s_prev, acc):
    c = w.shape[2]
    rim = 4 * side
    spread(side, acc, d[: side * side], w, c, 2 * c, 0, c, True)
    own, edge = gather_frame(side, acc)
    inner[...] = own
    picked = dot(rim_sel[...], edge).astype(BF)
    s_next[...] = picked[: rim // 2]
    s_prev[...] = picked[rim // 2 :]


def back_early_kernel(side, d, d_u, wc, wg, acc):
    c = wc.shape[2]
    cells = side * side
    acc[...] = jnp.zeros_like(acc)
    for a in range(3):
        for b in range(3):
            rows = slice(a * side, a * side + cells)
            t = a * 3 + b
            acc[b, rows, :c] += dot_nt(d[:cells], wc[t, :c, :]) + dot_nt(d_u[:cells], wg[t, :c, :c])
            acc[b, rows, c:] += dot_nt(d_u[:cells], wg[t, c:, :c])


def reset_kernel(side, inner, rp, rn, place, gate, h, g, d_c, d, direct):
    c = g.shape[1]
    d_rh = inner[...] + dot(place[...], jnp.concatenate([rp[...], rn[...]], axis=0))
    update, reset = gate[:, :c], gate[:, c:]
    cells = side * side
    d[:cells] = d_c[...]
    d[cells:] = (d_rh * h[:, c:].astype(F32) * reset * (1.0 - reset)).astype(BF)
    direct[...] = g[...].astype(F32) * (1.0 - update) + d_rh * reset


def back_gate_kernel(side, early, d, w, direct, rim_sel, inner, s_next, s_prev, acc):
    c = d.shape[1]
    rim = 4 * side
    acc[...] = early[...]
    cells = side * side
    spread(side, acc, d[cells:], w, 0, 2 * c, c, 2 * c, False)
    own, edge = gather_frame(side, acc)
    inner[:, :c] = own[:, :c]
    inner[:, c:] = own[:, c:] + direct[...]
    picked = dot(rim_sel[...], edge).astype(BF)
    s_next[...] = picked[: rim // 2]
    s_prev[...] = picked[rim // 2 :]


def final_kernel(inner, rp, rn, place, gx, gh):
    c = gx.shape[1]
    total = inner[...] + dot(place[...], jnp.concatenate([rp[...], rn[...]], axis=0))
    gx[...] = total[:, :c].astype(BF)
    gh[...] = total[:, c:].astype(BF)


def near_reset_kernel(side, *refs):
    x, packs, (m0, m2, w, bias, taps_in, out, taps, f, sems) = refs[1:4], refs[5:8], refs[8:]
    (copy,) = start_loads([(taps_in, taps)], sems)
    cells, rim, c = side * side, 4 * side, out.shape[2]
    for n in range(3):
        tile = jnp.concatenate([x[n][...], packs[n][:cells]], axis=1)
        strips = [packs[n][cells + k * rim : cells + (k + 1) * rim] for k in range(2 * c // 128)]
        strips = jnp.concatenate(strips, axis=1)
        frames(side, tile, strips, m0, m2, f.at[n])
    cols = [
        jnp.concatenate([f[n, b, a * side : a * side + cells, :] for n in range(3)], axis=0)
        for a in range(3)
        for b in range(3)
    ]
    rows = [w[t, :, c:] for t in range(9)]
    reset = jax.nn.sigmoid(dot(jnp.concatenate(cols, axis=1), jnp.concatenate(rows, axis=0)) + bias[:, c:])
    for n in range(3):
        out[n] = (reset[n * cells : (n + 1) * cells] * jnp.concatenate([x[n][:, c:], packs[n][:cells]], axis=1).astype(F32)).astype(BF)
    copy.wait()


def lhs_kernel(side, rows, tiles, cand, *refs):
    x, packs, more = refs[:4], refs[4:8], refs[8:-4]
    me = lax.axis_index("tile")
    taps, out, src, turned = refs[-4:]
    cells, rim = side * side, 4 * side
    c = (x[0].shape[1] + 128) // 2
    per_tap = 2 * c // 128
    for n in range(4):
        lanes = slice(n * 128, (n + 1) * 128)
        for k in range(per_tap):
            at = slice(k * 128, (k + 1) * 128)
            col = slice(at.start % c, at.start % c + 128)
            if cand and at.start >= c:
                rh, rh_near, ds = more[0], more[1], more[2:]
                src[k, :cells, lanes] = rh[:, col] if n == 0 else rh_near[n - 1, :, col]
                src[k, cells:, lanes] = ds[n][cells:, col]
            else:
                src[k, :cells, lanes] = x[n][:, at] if k < per_tap - 1 else packs[n][:cells]
                src[k, cells:, lanes] = packs[n][cells + k * rim : cells + (k + 1) * rim]
    for k in range(per_tap):
        turned[k] = src[k].T
    for t in range(out.shape[0]):
        target = me ^ (8 * (t // 2) + t % 2)
        for n in range(out.shape[1] // 128):
            block = jnp.minimum(target * rows // 128 + n, 9 * per_tap - 1)
            part = dot(turned[block % per_tap], taps[block // per_tap]).astype(BF)
            for k in range(4):
                out[t, n * 128 : (n + 1) * 128, k * cells : (k + 1) * cells] = part[k * 128 : (k + 1) * 128]


def weight_kernel(side, rows, parts, *refs):
    n = len(parts)
    lhs, ds, keep, sends, acc = refs[:n], refs[n : n + 4], refs[n + 4], refs[n + 5 : -1], refs[-1]
    cells = side * side
    c, width = ds[0].shape[1], sends[0].shape[2]
    me = lax.axis_index("tile")
    right = [jnp.concatenate([d[k * cells : (k + 1) * cells] for d in ds], axis=0) for k in parts]
    for t in range(lhs[0].shape[0]):
        target = me ^ (8 * (t // 2) + t % 2)
        first = pl.multiple_of(target * rows % 128, 8)
        for k in range(n):
            acc[k, t % 2] = dot(lhs[k][t], right[k])
            part = acc[k, t % 2, pl.ds(first, rows), :]
            if t % 2 == 0:
                keep[t // 2, :, k * c : (k + 1) * c] = part
            else:
                for j in range(c // width):
                    sends[k * (c // width) + j][t // 2] = part[:, j * width : (j + 1) * width].astype(BF)


def pair_kernel(*refs):
    own, far = refs[-2:]
    keep, first, at = None, 0, 0
    for r in refs[:-2]:
        if r.dtype == F32:
            keep, at = r, 0
            continue
        c = r.shape[2]
        cols = slice(first, first + c)
        own[:, cols] = keep[0, :, at : at + c] + r[0].astype(F32)
        for m in range(1, keep.shape[0]):
            far[m - 1, :, cols] = (keep[m, :, at : at + c] + r[m].astype(F32)).astype(BF)
        at, first = at + c, first + c


def sum_kernel(*refs):
    total = refs[0][...]
    for r in refs[1:-1]:
        total += r[...].astype(F32)
    refs[-1][...] = total


def sum_gate_kernel(update, *refs):
    parts, gate = refs[:-1], refs[-1]
    c = update.shape[1]
    total = parts[0][...]
    for r in parts[1:]:
        total += r[...].astype(F32)
    gate[:, :c] = update[...]
    gate[:, c:] = total


def shards(
    x_tiles, h_tiles, grad_out, w_gate, b_gate, w_cand, b_cand, partner_edge, edge_flip, tile_slot
):
    side, c = x_tiles.shape[1], x_tiles.shape[3]
    tiles = lax.axis_size("tile")
    cells, rim = side * side, 4 * side
    half, band = rim // 2, (side + 2) * side
    rows = 18 * c // tiles
    groups = tiles // 8
    blocks = max((rows * j + rows - 1) // 128 - rows * j // 128 + 1 for j in range(tiles)) * 128
    x, h, g = (u.reshape(cells, c) for u in (x_tiles, h_tiles, grad_out))
    wg, wc = w_gate.reshape(9, 2 * c, 2 * c), w_cand.reshape(9, 2 * c, c)
    bg, bc = b_gate.reshape(1, 2 * c), b_cand.reshape(1, c)
    m = frame_matrices(side)
    m0, m2 = jnp.asarray(m[0], BF), jnp.asarray(m[2], BF)
    taps = jnp.asarray(tap_matrices(side), BF)
    cross = [(i, (i + 1) % tiles if i % 2 else (i - 1) % tiles) for i in range(tiles)]
    ran = []

    def run(name, body, outs, *args, **options):
        if ran:
            args = (after(args[0], ran[-1]),) + args[1:]
        with jax.named_scope(name):
            results = call(body, outs, *args, **options)
        ran.append(results[0])
        return results

    def load(name, *args):
        n = len(args)
        return run(
            name, functools.partial(load_kernel, n), [(a.shape, a.dtype) for a in args], *args,
            hbm=range(n), scratch=[pltpu.SemaphoreType.DMA((n,))],
        )

    def after(u, *others):
        return lax.optimization_barrier((u,) + others)[0]

    def swap(u, k):
        return lax.ppermute(u, "tile", [(i, i ^ k) for i in range(tiles)])

    def exchange(s_first, s_second):
        return swap(s_first, 1), lax.ppermute(s_second, "tile", cross)

    def near(u):
        return [u] + [swap(u, k) for k in (2, 4, 6)]

    def lhs_of(name, cand, *args, cost=0):
        return run(
            name, functools.partial(lhs_kernel, side, rows, tiles, cand),
            [((2 * groups, blocks, 4 * cells), BF)],
            *args, taps_v,
            scratch=[
                pltpu.VMEM((2 * c // 128, cells + rim, 512), BF),
                pltpu.VMEM((2 * c // 128, 512, cells + rim), BF),
            ],
            cost=cost,
        )[0]

    def products(name, parts, lhs, ds, cuts=1, cost=0):
        n = len(parts)
        keep, *sends = run(
            name, functools.partial(weight_kernel, side, rows, parts),
            [((groups, rows, n * c), F32)] + [((groups, rows, c // cuts), BF)] * (n * cuts),
            *lhs, *ds,
            scratch=[pltpu.VMEM((n, 2, blocks, c), F32)],
            cost=cost,
        )
        return [keep] + [swap(u, 1) for u in sends]

    def pair(name, *sums, cost=0):
        n = sum(u.shape[2] for u in sums if u.dtype == F32)
        own, far = run(
            name, pair_kernel, [((rows, n), F32), ((groups - 1, rows, n), BF)], *sums, cost=cost
        )
        return [own] + [swap(far[k - 1], 8 * k) for k in range(1, groups)]

    xh, front, s1n, s1p, sel, place, turn, rim_sel = run(
        "route", functools.partial(route_kernel, side, tiles),
        [
            ((cells, 2 * c), BF),
            ((cells, 2 * c - 128), BF),
            ((half, 2 * c), BF),
            ((half, 2 * c), BF),
            ((rim, cells), BF),
            ((cells, rim), BF),
            ((rim, rim), BF),
            ((rim, 2 * side + 2 * cells), BF),
        ],
        partner_edge.T, edge_flip.T, tile_slot, x, h,
        hbm=(0, 1, 2, 3, 4),
        scratch=[
            pltpu.SMEM((4, tiles), jnp.int32),
            pltpu.SMEM((4, tiles), jnp.int32),
            pltpu.SMEM((tiles,), jnp.int32),
            pltpu.SemaphoreType.DMA((7,)),
        ],
    )
    r1p, r1n = exchange(s1n, s1p)
    x_near = near(front)
    wg_v, m0, m2, bg_v = load("load_gate", wg, m0, m2, bg)
    gate, rh, pack, s2n, s2p, f, wc_v, bc_v, g_v = run(
        "gate", functools.partial(gate_kernel, side),
        [
            ((cells, 2 * c), F32),
            ((cells, c), BF),
            ((cells + 2 * c // 128 * rim, 128), BF),
            ((half, c), BF),
            ((half, c), BF),
            ((3, band, 2 * c), BF),
            (wc.shape, BF),
            (bc.shape, F32),
            (g.shape, BF),
        ],
        xh, r1p, r1n, turn, m0, m2, wg_v, bg_v, sel, wc, bc, g,
        hbm=(9, 10, 11), scratch=[pltpu.SemaphoreType.DMA((3,))], cost=5,
    )
    r2p, r2n = exchange(s2n, s2p)
    pack_near = near(after(pack, *x_near))
    (acc_x,) = run("cand_x", functools.partial(cand_x_kernel, side), [((cells, c), F32)], after(f, *x_near), wc_v, bc_v)
    d_c, d_u, _ = run(
        "cand", functools.partial(cand_kernel, side),
        [((cells, c), BF), ((cells + rim, c), BF), ((3, band, c), BF)],
        acc_x, rh, r2p, r2n, turn, m0, m2, wc_v, gate, xh, g_v, cost=3,
    )
    inner_rh, s3n, s3p, _ = run(
        "back_rh", functools.partial(back_rh_kernel, side),
        [((cells, c), F32), ((half, c), BF), ((half, c), BF), ((3, band, c), F32)],
        d_c, wc_v, rim_sel,
    )
    r3p, r3n = exchange(s3n, s3p)
    u_near = near(d_u)
    rh_near, taps_v = run(
        "near_reset", functools.partial(near_reset_kernel, side), [((3, cells, c), BF), (taps.shape, BF)],
        *x_near, *pack_near, m0, m2, wg_v, bg_v, taps,
        hbm=(12,),
        scratch=[pltpu.VMEM((3, 3, band, 2 * c), BF), pltpu.SemaphoreType.DMA((1,))], cost=0,
    )
    d_cr, direct = run(
        "reset", functools.partial(reset_kernel, side),
        [((2 * cells, c), BF), ((cells, c), F32)],
        inner_rh, r3p, r3n, place, gate, xh, g_v, d_c, cost=5,
    )
    d_near = near(d_cr)
    lhs_gate = lhs_of("lhs_gate", False, *x_near, *pack_near, cost=0)
    sums_u = products("weights_update", (0,), [lhs_gate], u_near, cuts=2, cost=0)
    lhs_cand = lhs_of("lhs_cand", True, *x_near, *pack_near, rh, rh_near, *u_near, cost=0)
    parts_u = pair("pair_update", *sums_u)
    (early,) = run(
        "back_early", functools.partial(back_early_kernel, side), [((3, band, 2 * c), F32)], d_c, d_u, wc_v, wg_v
    )
    inner, s4n, s4p, _ = run(
        "back_gate", functools.partial(back_gate_kernel, side),
        [((cells, 2 * c), F32), ((half, 2 * c), BF), ((half, 2 * c), BF), ((3, band, 2 * c), F32)],
        early, d_cr, wg_v, direct, rim_sel,
    )
    r4p, r4n = exchange(s4n, s4p)
    sums_r = products("weights_reset", (1,), [lhs_gate], d_near, cuts=1, cost=0)
    sums_c = products("weights_cand", (0,), [lhs_cand], d_near, cuts=2, cost=0)
    (sum_u,) = run("sum_update", sum_kernel, [((rows, c), F32)], *parts_u, cost=2)
    parts_r = pair("pair_reset", *sums_r)
    parts_c = pair("pair_cand", *sums_c)
    (grad_w_gate,) = run(
        "sum_gate", sum_gate_kernel, [((rows, 2 * c), F32)], sum_u, *parts_r, pin=False, cost=0
    )
    gx, gh = run(
        "final", final_kernel, [((cells, c), BF), ((cells, c), BF)], inner, r4p, r4n, place, pin=False, cost=3
    )
    (grad_w_cand,) = run("sum_cand", sum_kernel, [((rows, c), F32)], *parts_c, pin=False)
    shape = (1, side, side, c)
    return gx.reshape(shape), gh.reshape(shape), grad_w_gate, grad_w_cand


def solution(mesh):
    tile = P(("grp", "tile"), None, None, None)
    rows = P(("grp", "tile"), None)
    return jax.shard_map(
        shards,
        mesh=mesh,
        in_specs=(tile, tile, tile) + (P(),) * 7,
        out_specs=(tile, tile, rows, rows),
        check_vma=False,
    )
```
